32 devices in a mesh: band: 4 (over z), dev: 8 (over y, x, core).
Axes of the slice: x: 2, y: 2, z: 4, core: 2. Of those that a mesh axis runs over, the one named last changes fastest.
Arguments:
- anomaly: float32 [256, 131072], P('dev', 'band'), may hold values from -6 to 6
- ocean_mask: int32 [131072], P('band'), may hold values 0 or 1
- area_weight: float32 [131072], P('band'), may hold values from 0.02 to 1
Outputs:
- factor: float32 [256, 256], replicated
- scores: float32 [256, 131072], P(None, ('band', 'dev'))
The draws below stay inside these ranges and needn't reach their ends.
All inputs are finite; a program needn't handle non-finite values. No bound on the sum of `ocean_mask` on one device may be relied on, other than what follows from the above.
Results may differ from the reference program's by a relative error of at most 0.000075.
Values sent between devices are 32-bit elements; how exact they have to be, the bound alone decides.
No kernel may reach another device: no remote copies, remote signals or barrier semaphores. Data moves between devices by JAX's collectives and lax.ppermute only.
A program may use at most 64 MiB of HBM per device.

```python
import math
import jax
import jax.numpy as jnp
from jax import lax

SNAPS = 256
CELLS = 131072


def place_ends(array, rng, least, top_value):
    dims = array.shape
    index_at = [jax.random.randint(jax.random.fold_in(rng, axis), (), 0, dims[axis]) for axis in range(len(dims))]
    array = array.at[tuple(index_at)].set(least)
    longest = dims.index(max(dims))
    index_at[longest] = (index_at[longest] + 1) % dims[longest]
    return array.at[tuple(index_at)].set(top_value)


def steps_of(rng, dims, cuts, low, largest):
    factor_of, own = 1.0, jax.random.fold_in(rng, 6)
    for axis_at, blocks in cuts:
        steps = jnp.exp(jax.random.uniform(jax.random.fold_in(own, axis_at), (blocks,), jnp.float32, low / len(cuts), largest / len(cuts)))
        factor_of = factor_of * jnp.repeat(steps, dims[axis_at] // blocks).reshape([-1 if axis == axis_at else 1 for axis in range(len(dims))])
    return factor_of


def normal_values(own_key, extent, spread, limit, shards=(), kind=jnp.bfloat16):
    gain = steps_of(own_key, extent, shards, -0.22, 0.18) if shards else 1.0
    array = jax.random.normal(own_key, extent, jnp.float32) * spread * gain
    return jnp.minimum(jnp.maximum(array, -limit), limit).astype(kind)


def setup_inputs(seed: int = 0) -> dict:
    splits = jax.random.split(jax.random.key(seed), 4)
    anomaly = normal_values(splits[0], (SNAPS, CELLS), 1.0, 6.0, ((0, 8), (1, 4)), jnp.float32)
    ocean_mask = place_ends((jax.random.randint(splits[1], (CELLS,), 0, 3) < 2).astype(jnp.int32), jax.random.fold_in(splits[1], 1), 0, 1)
    area_weight = jnp.clip(jnp.exp(math.log(1.0) - 3.912023 * jax.random.uniform(splits[2], (CELLS,), jnp.float32) ** steps_of(splits[2], (CELLS,), ((0, 4),), -0.2, 0.2)), 0.02, 1.0)
    return {"anomaly": anomaly, "ocean_mask": ocean_mask, "area_weight": area_weight}


def reference(anomaly, ocean_mask, area_weight):
    weights = area_weight * ocean_mask.astype(jnp.float32)
    scaled = anomaly * jnp.sqrt(weights)[None, :]
    total = jnp.sum(weights)
    gram = jnp.dot(scaled, scaled.T, precision=lax.Precision.HIGHEST)
    lower = jnp.linalg.cholesky(gram / total)
    scores = lax.linalg.triangular_solve(lower, scaled, left_side=True, lower=True)
    return (lower.T, scores)
```

```python
import functools
import jax
import jax.numpy as jnp
from jax import lax
from jax.experimental import pallas as pl
from jax.experimental.pallas import tpu as pltpu
from jax.sharding import PartitionSpec as P

F32, BF16 = jnp.float32, jnp.bfloat16
SUB, LANE = 8, 128
PANEL = 64
NN = (((1,), (0,)), ((), ()))
NT = (((1,), (1,)), ((), ()))
VMEM_LIMIT = 32 * 1024 * 1024


def split2(x):
    high = x.astype(BF16)
    return high, (x - high.astype(F32)).astype(BF16)


def split3(x):
    high = x.astype(BF16)
    rest = x - high.astype(F32)
    middle = rest.astype(BF16)
    return high, middle, (rest - middle.astype(F32)).astype(BF16)


def dot(a, b, dims):
    return lax.dot_general(a, b, dims, preferred_element_type=F32)


def product(a, b, dims):
    a1, a2, a3 = a
    b1, b2, b3 = b
    small = (dot(a1, b3, dims) + dot(a3, b1, dims)) + dot(a2, b2, dims)
    return dot(a1, b1, dims) + ((dot(a1, b2, dims) + dot(a2, b1, dims)) + small)


def tree_sum(terms):
    while len(terms) > 1:
        terms = [sum(terms[i : i + 2][1:], terms[i]) for i in range(0, len(terms), 2)]
    return terms[0]


def row_of(x, k):
    return jnp.broadcast_to(x[k : k + 1, :], (SUB, LANE))


def column_of(x, k):
    return jnp.broadcast_to(x[:, k : k + 1], (SUB, LANE))


def factor_panel(tiles, start):
    tiles = list(tiles)
    count = len(tiles)
    sub = lax.broadcasted_iota(jnp.int32, (SUB, LANE), 0)
    diag = [column_of(tiles[0], start + k) for k in range(SUB)]
    for b in range(count):
        rest = range(b + 1, count)
        cols = {t: [column_of(tiles[t], start + SUB * b + k) for k in range(SUB)] for t in rest}
        ahead = [column_of(tiles[b + 1], start + SUB * (b + 1) + k) for k in range(SUB)] if b + 1 < count else None
        rows = []
        for j in range(SUB):
            inverse = lax.rsqrt(row_of(diag[j], j))
            own = diag[j] * inverse
            spread = {k: row_of(own, k) for k in range(j + 1, SUB)}
            for k in range(j + 1, SUB):
                diag[k] = diag[k] - own * spread[k]
            for t in rest:
                cols[t][j] = cols[t][j] * inverse
                for k in range(j + 1, SUB):
                    cols[t][k] = cols[t][k] - cols[t][j] * spread[k]
            row = row_of(tiles[b], j) * inverse
            tiles[b] = jnp.where(sub == j, row, jnp.where(sub > j, tiles[b] - own * row, tiles[b]))
            rows.append(row)
        if ahead is not None:
            below = cols[b + 1]
            diag = [ahead[k] - tree_sum([below[j] * row_of(below[j], k) for j in range(SUB)]) for k in range(SUB)]
        for t in rest:
            tiles[t] = tiles[t] - tree_sum([cols[t][j] * rows[j] for j in range(SUB)])
    return tiles


def cholesky_and_inverse(a_ref, inverse_ref, upper_ref):
    order = a_ref.shape[0]
    inverse_ref[...] = jnp.zeros((order, order), F32)
    upper_ref[...] = jnp.zeros((order, order), F32)
    lane = lax.broadcasted_iota(jnp.int32, (SUB, LANE), 1)
    sub = lax.broadcasted_iota(jnp.int32, (SUB, LANE), 0)
    block_row = lax.broadcasted_iota(jnp.int32, (PANEL, PANEL), 0)
    block_col = lax.broadcasted_iota(jnp.int32, (PANEL, PANEL), 1)
    for first in range(0, order, PANEL):
        end = first + PANEL
        start = first % LANE
        other = PANEL - start
        tiles = []
        for t in range(PANEL // SUB):
            at = first + SUB * t
            eye = jnp.where(lane - other == sub + SUB * t, 1.0, 0.0)
            inside = (lane >= start) & (lane < start + PANEL)
            tiles.append(jnp.where(inside, a_ref[at : at + SUB, first - start : first - start + LANE], eye))
        both = jnp.concatenate(factor_panel(tiles, start), 0)
        upper_ref[first:end, first:end] = jnp.where(block_col >= block_row, both[:, start : start + PANEL], 0.0)
        own = both[:, other : other + PANEL]
        own_terms = split3(own)
        if first:
            inverse_ref[first:end, :first] = product(own_terms, split3(inverse_ref[first:end, :first]), NN)
        inverse_ref[first:end, first:end] = own
        if end < order:
            lower = product(split3(a_ref[end:, first:end]), own_terms, NT)
            lower_terms = split3(lower)
            a_ref[end:, end:] = a_ref[end:, end:] - product(lower_terms, lower_terms, NT)
            inverse_ref[end:, :end] = inverse_ref[end:, :end] - product(lower_terms, split3(inverse_ref[first:end, :end]), NN)
            upper_ref[first:end, end:] = lower.T


def slice_kernel(index_ref, x_ref, out_ref):
    out_ref[...] = x_ref[...]


def take_cells(anomaly, index, cells):
    rows = anomaly.shape[0]
    return pl.pallas_call(
        slice_kernel,
        grid_spec=pltpu.PrefetchScalarGridSpec(
            num_scalar_prefetch=1,
            grid=(1,),
            in_specs=[pl.BlockSpec((rows, cells), lambda i, at: (0, at[0]))],
            out_specs=pl.BlockSpec((rows, cells), lambda i, at: (0, 0)),
        ),
        out_shape=jax.ShapeDtypeStruct((rows, cells), F32),
        compiler_params=pltpu.CompilerParams(vmem_limit_bytes=VMEM_LIMIT),
    )(index[None], anomaly)


def gram_kernel(pieces, me_ref, own_ref, *refs):
    piece_refs, (root_ref, total_ref) = refs[: pieces - 1], refs[pieces - 1 : pieces + 1]
    high_ref, low_ref, keep_ref, send_ref, scaled_ref, main_ref, cross_ref = refs[pieces + 1 :]
    step = pl.program_id(0)
    me = me_ref[0]
    rows = own_ref.shape[0]
    root = root_ref[...]
    for k, ref in enumerate((own_ref, *piece_refs)):
        at = pl.multiple_of((me ^ k) * rows, rows)
        scaled_ref[pl.ds(at, rows), :] = ref[...] * root
    high, low = split2(scaled_ref[...])
    high_ref[...] = high
    low_ref[...] = low

    @pl.when(step == 0)
    def _():
        main_ref[...] = jnp.zeros_like(main_ref)
        cross_ref[...] = jnp.zeros_like(cross_ref)

    main_ref[...] += dot(high, high, NT)
    cross_ref[...] += dot(high, low, NT)

    @pl.when(step == pl.num_programs(0) - 1)
    def _():
        cross = cross_ref[...]
        main_ref[...] = main_ref[...] + (cross + cross.T)
        half = main_ref.shape[0] // 2
        row = lax.broadcasted_iota(jnp.int32, (half, half), 0)
        col = lax.broadcasted_iota(jnp.int32, (half, half), 1)
        last = main_ref[half:, half:]
        both = jnp.where(row >= col, main_ref[:half, :half], last)
        corner = jnp.sum(jnp.where(row == col, last, 0.0), axis=0, keepdims=True)
        extra_row = lax.broadcasted_iota(jnp.int32, (SUB, half), 0)
        extra = jnp.where(extra_row == 0, jnp.broadcast_to(corner, (SUB, half)), jnp.broadcast_to(total_ref[...], (SUB, half)))
        off = main_ref[half:, :half]
        first_core = (me & 1) == 0
        for ref, is_off in ((keep_ref, first_core), (send_ref, jnp.logical_not(first_core))):
            ref[:half, :] = jnp.where(is_off, off, both)
            ref[half:, :] = extra


def form_gram(me, anomaly, pieces, root, total, cells):
    rows = anomaly.shape[0]
    count = len(pieces) + 1
    order = rows * count
    step = min(cells, 1024)
    packed = (order // 2 + SUB, order // 2)
    steps = cells // step
    return pl.pallas_call(
        functools.partial(gram_kernel, count),
        grid_spec=pltpu.PrefetchScalarGridSpec(
            num_scalar_prefetch=1,
            grid=(steps,),
            in_specs=[pl.BlockSpec((rows, step), lambda i, me: (0, me[0] * steps + i))]
            + [pl.BlockSpec((rows, step), lambda i, me: (0, i))] * (count - 1)
            + [pl.BlockSpec((1, step), lambda i, me: (0, i)), pl.BlockSpec((1, 1), lambda i, me: (0, 0))],
            out_specs=[pl.BlockSpec((order, step), lambda i, me: (0, i))] * 2
            + [pl.BlockSpec(packed, lambda i, me: (0, 0))] * 2,
            scratch_shapes=[pltpu.VMEM((order, step), F32), pltpu.VMEM((order, order), F32), pltpu.VMEM((order, order), F32)],
        ),
        out_shape=[jax.ShapeDtypeStruct((order, cells), BF16)] * 2 + [jax.ShapeDtypeStruct(packed, F32)] * 2,
        compiler_params=pltpu.CompilerParams(vmem_limit_bytes=VMEM_LIMIT),
        cost_estimate=pl.CostEstimate(flops=4 * order * order * cells, bytes_accessed=8 * order * cells, transcendentals=0),
    )(me[None], anomaly, *pieces, root, total)


def solve_kernel(me_ref, mine_ref, other_ref, high_ref, low_ref, upper_ref, scores_ref, a_ref, inverse_ref, high_inv_ref, low_inv_ref):
    @pl.when(pl.program_id(0) == 0)
    def _():
        half = mine_ref.shape[1]
        first_core = (me_ref[0] & 1) == 0
        mine, other = mine_ref[...], other_ref[...]
        off = jnp.where(first_core, mine[:half], other[:half])
        both = jnp.where(first_core, other[:half], mine[:half])
        scale = 1.0 / mine[half + 1 : half + 2, :]
        row = lax.broadcasted_iota(jnp.int32, (half, half), 0)
        col = lax.broadcasted_iota(jnp.int32, (half, half), 1)
        turned = both.T
        corner = jnp.broadcast_to(mine[half : half + 1, :], (half, half))
        a_ref[:half, :half] = jnp.where(row >= col, both, turned) * scale
        a_ref[half:, half:] = jnp.where(row < col, both, jnp.where(row > col, turned, corner)) * scale
        a_ref[half:, :half] = off * scale
        cholesky_and_inverse(a_ref, inverse_ref, upper_ref)
        high, low = split2(inverse_ref[...])
        high_inv_ref[...] = high
        low_inv_ref[...] = low

    high = high_inv_ref[...]
    scores_ref[...] = dot(high, high_ref[...], NN) + (dot(high, low_ref[...], NN) + dot(low_inv_ref[...], high_ref[...], NN))


def solve(me, mine, other, high, low):
    order, cells = high.shape
    step = min(cells, 512)
    whole = lambda i, me: (0, 0)
    chunk = lambda i, me: (0, i)
    return pl.pallas_call(
        solve_kernel,
        grid_spec=pltpu.PrefetchScalarGridSpec(
            num_scalar_prefetch=1,
            grid=(cells // step,),
            in_specs=[pl.BlockSpec(mine.shape, whole)] * 2 + [pl.BlockSpec((order, step), chunk)] * 2,
            out_specs=[pl.BlockSpec((order, order), whole), pl.BlockSpec((order, step), chunk)],
            scratch_shapes=[pltpu.VMEM((order, order), F32)] * 2 + [pltpu.VMEM((order, order), BF16)] * 2,
        ),
        out_shape=[jax.ShapeDtypeStruct((order, order), F32), jax.ShapeDtypeStruct((order, cells), F32)],
        compiler_params=pltpu.CompilerParams(vmem_limit_bytes=VMEM_LIMIT),
        cost_estimate=pl.CostEstimate(flops=6 * order * order * cells, bytes_accessed=8 * order * cells, transcendentals=0),
    )(me[None], mine, other, high, low)


def swap(x, axis, mask):
    return lax.ppermute(x, axis, [(i, i ^ mask) for i in range(lax.axis_size(axis))])


def sum_over(x, axis, first):
    size = lax.axis_size(axis)
    while first < size:
        if 2 * first < size:
            near, far, both = swap(x, axis, first), swap(x, axis, 2 * first), swap(x, axis, 3 * first)
            x = (x + near) + (far + both)
        else:
            x = x + swap(x, axis, first)
        first *= 4
    return x


def on_device(anomaly, ocean_mask, area_weight):
    size = lax.axis_size("dev")
    me = lax.axis_index("dev")
    cells = anomaly.shape[1] // size
    order = sorted(range(1, size), key=lambda k: (-(k >> 1).bit_count(), k & 1))
    pieces = {k: swap(take_cells(anomaly, me ^ k, cells), "dev", k) for k in order}
    own = lambda x: lax.dynamic_slice_in_dim(x, me * cells, cells, 0)
    weights = own(area_weight) * own(ocean_mask).astype(F32)
    root = jnp.sqrt(weights)[None, :]
    total = jnp.sum(weights)[None, None]
    high, low, keep, send = form_gram(me, anomaly, [pieces[k] for k in range(1, size)], root, total, cells)
    mine = keep + swap(send, "dev", 1)
    mine = sum_over(mine, "dev", 2)
    mine = sum_over(mine, "band", 1)
    other = swap(mine, "dev", 1)
    return tuple(solve(me, mine, other, high, low))


def solution(mesh):
    return jax.shard_map(
        on_device,
        mesh=mesh,
        in_specs=(P("dev", "band"), P("band"), P("band")),
        out_specs=(P(), P(None, ("band", "dev"))),
        check_vma=False,
    )
```

```python
import functools
import jax
import jax.numpy as jnp
from jax import lax
from jax.experimental import pallas as pl
from jax.experimental.pallas import tpu as pltpu
from jax.sharding import PartitionSpec as P

F32, BF16 = jnp.float32, jnp.bfloat16
SUB, LANE = 8, 128
PANEL = 64
NN = (((1,), (0,)), ((), ()))
NT = (((1,), (1,)), ((), ()))
VMEM_LIMIT = 24 * 1024 * 1024
STEP = 512


def split2(x):
    high = x.astype(BF16)
    return high, (x - high.astype(F32)).astype(BF16)


def split3(x):
    high = x.astype(BF16)
    rest = x - high.astype(F32)
    middle = rest.astype(BF16)
    return high, middle, (rest - middle.astype(F32)).astype(BF16)


def dot(a, b, dims):
    return lax.dot_general(a, b, dims, preferred_element_type=F32)


def product(a, b, dims):
    a1, a2, a3 = a
    b1, b2, b3 = b
    small = (dot(a1, b3, dims) + dot(a3, b1, dims)) + dot(a2, b2, dims)
    return dot(a1, b1, dims) + ((dot(a1, b2, dims) + dot(a2, b1, dims)) + small)


def tree_sum(terms):
    while len(terms) > 1:
        terms = [sum(terms[i : i + 2][1:], terms[i]) for i in range(0, len(terms), 2)]
    return terms[0]


def row_of(x, k):
    return jnp.broadcast_to(x[k : k + 1, :], (SUB, LANE))


def column_of(x, k):
    return jnp.broadcast_to(x[:, k : k + 1], (SUB, LANE))


def factor_panel(tiles, start):
    tiles = list(tiles)
    count = len(tiles)
    sub = lax.broadcasted_iota(jnp.int32, (SUB, LANE), 0)
    diag = [column_of(tiles[0], start + k) for k in range(SUB)]
    for b in range(count):
        rest = range(b + 1, count)
        cols = {t: [column_of(tiles[t], start + SUB * b + k) for k in range(SUB)] for t in rest}
        ahead = [column_of(tiles[b + 1], start + SUB * (b + 1) + k) for k in range(SUB)] if b + 1 < count else None
        rows = []
        for j in range(SUB):
            inverse = lax.rsqrt(row_of(diag[j], j))
            own = diag[j] * inverse
            spread = {k: row_of(own, k) for k in range(j + 1, SUB)}
            for k in range(j + 1, SUB):
                diag[k] = diag[k] - own * spread[k]
            for t in rest:
                cols[t][j] = cols[t][j] * inverse
                for k in range(j + 1, SUB):
                    cols[t][k] = cols[t][k] - cols[t][j] * spread[k]
            row = row_of(tiles[b], j) * inverse
            tiles[b] = jnp.where(sub == j, row, jnp.where(sub > j, tiles[b] - own * row, tiles[b]))
            rows.append(row)
        if ahead is not None:
            below = cols[b + 1]
            diag = [ahead[k] - tree_sum([below[j] * row_of(below[j], k) for j in range(SUB)]) for k in range(SUB)]
        for t in rest:
            tiles[t] = tiles[t] - tree_sum([cols[t][j] * rows[j] for j in range(SUB)])
    return tiles


def cholesky_and_inverse(a_ref, inverse_ref, upper_ref, lower_ref):
    order = a_ref.shape[0]
    inverse_ref[...] = jnp.zeros((order, order), F32)
    upper_ref[...] = jnp.zeros((order, order), F32)
    lane = lax.broadcasted_iota(jnp.int32, (SUB, PANEL), 1)
    sub = lax.broadcasted_iota(jnp.int32, (SUB, PANEL), 0)
    block_row = lax.broadcasted_iota(jnp.int32, (PANEL, PANEL), 0)
    block_col = lax.broadcasted_iota(jnp.int32, (PANEL, PANEL), 1)
    for first in range(0, order, PANEL):
        end = first + PANEL
        column = a_ref[first:, first:end]
        if first:
            done = split3(lower_ref[first:, :first])
            column = column - product(done, tuple(term[:PANEL] for term in done), NT)
        tiles = []
        for t in range(PANEL // SUB):
            eye = jnp.where(lane == sub + SUB * t, 1.0, 0.0)
            tiles.append(jnp.concatenate([column[SUB * t : SUB * t + SUB], eye], 1))
        both = jnp.concatenate(factor_panel(tiles, 0), 0)
        upper_ref[first:end, first:end] = jnp.where(block_col >= block_row, both[:, :PANEL], 0.0)
        own = both[:, PANEL:]
        own_terms = split3(own)
        if end < order:
            lower = product(split3(column[PANEL:]), own_terms, NT)
            lower_ref[end:, first:end] = lower
            upper_ref[first:end, end:] = lower.T
        if first:
            behind = product(tuple(term[:PANEL] for term in done), split3(inverse_ref[:first, :first]), NN)
            inverse_ref[first:end, :first] = -product(own_terms, split3(behind), NN)
        inverse_ref[first:end, first:end] = own


def gram_kernel(pieces, me_ref, own_ref, *refs):
    piece_refs, (root_ref, total_ref) = refs[: pieces - 1], refs[pieces - 1 : pieces + 1]
    high_ref, low_ref, keep_ref, send_ref, scaled_ref, sum_ref = refs[pieces + 1 :]
    me = me_ref[0]
    rows, cells = own_ref.shape
    main = cross = None
    for first in range(0, cells, STEP):
        at = slice(first, min(first + STEP, cells))
        root = root_ref[:, at]
        for k, ref in enumerate((own_ref, *piece_refs)):
            scaled_ref[pl.ds(pl.multiple_of((me ^ k) * rows, rows), rows), at] = ref[:, at] * root
        high, low = split2(scaled_ref[:, at])
        high_ref[:, at] = high
        low_ref[:, at] = low
        more_main, more_cross = dot(high, high, NT), dot(high, low, NT)
        main, cross = (main + more_main, cross + more_cross) if first else (more_main, more_cross)
    sum_ref[...] = main + (cross + cross.T)
    half = sum_ref.shape[0] // 2
    row = lax.broadcasted_iota(jnp.int32, (half, half), 0)
    col = lax.broadcasted_iota(jnp.int32, (half, half), 1)
    last = sum_ref[half:, half:]
    both = jnp.where(row >= col, sum_ref[:half, :half], last)
    corner = jnp.sum(jnp.where(row == col, last, 0.0), axis=0, keepdims=True)
    extra_row = lax.broadcasted_iota(jnp.int32, (SUB, half), 0)
    extra = jnp.where(extra_row == 0, jnp.broadcast_to(corner, (SUB, half)), jnp.broadcast_to(total_ref[...], (SUB, half)))
    off = sum_ref[half:, :half]
    first_core = (me & 1) == 0
    for ref, is_off in ((keep_ref, first_core), (send_ref, jnp.logical_not(first_core))):
        ref[:half, :] = jnp.where(is_off, off, both)
        ref[half:, :] = extra


def form_gram(me, own, pieces, root, total):
    rows, cells = own.shape
    count = len(pieces) + 1
    order = rows * count
    packed = (order // 2 + SUB, order // 2)
    here = pl.BlockSpec(memory_space=pltpu.VMEM)
    return pl.pallas_call(
        functools.partial(gram_kernel, count),
        in_specs=[pl.BlockSpec(memory_space=pltpu.SMEM)] + [here] * (count + 2),
        out_specs=[here] * 4,
        out_shape=[jax.ShapeDtypeStruct((order, cells), BF16)] * 2 + [jax.ShapeDtypeStruct(packed, F32)] * 2,
        scratch_shapes=[pltpu.VMEM((order, cells), F32), pltpu.VMEM((order, order), F32)],
        compiler_params=pltpu.CompilerParams(vmem_limit_bytes=VMEM_LIMIT),
    )(me[None], own, *pieces, root, total)


def solve_kernel(me_ref, mine_ref, other_ref, *refs):
    term_refs, (upper_ref, scores_ref, out_ref, a_ref, inverse_ref, lower_ref, sems) = refs[:-7], refs[-7:]
    half = mine_ref.shape[1]
    first_core = (me_ref[0] & 1) == 0
    mine, other = mine_ref[...], other_ref[...]
    off = jnp.where(first_core, mine[:half], other[:half])
    both = jnp.where(first_core, other[:half], mine[:half])
    scale = 1.0 / mine[half + 1 : half + 2, :]
    row = lax.broadcasted_iota(jnp.int32, (half, half), 0)
    col = lax.broadcasted_iota(jnp.int32, (half, half), 1)
    turned = both.T
    corner = jnp.broadcast_to(mine[half : half + 1, :], (half, half))
    a_ref[:half, :half] = jnp.where(row >= col, both, turned) * scale
    a_ref[half:, half:] = jnp.where(row < col, both, jnp.where(row > col, turned, corner)) * scale
    a_ref[half:, :half] = off * scale
    cholesky_and_inverse(a_ref, inverse_ref, upper_ref, lower_ref)
    high, low = split2(inverse_ref[...])
    copies, at = [], 0
    for high_ref, low_ref in zip(term_refs[::2], term_refs[1::2]):
        for first in range(0, high_ref.shape[1], STEP):
            here = slice(first, min(first + STEP, high_ref.shape[1]))
            there = slice(at + here.start, at + here.stop)
            high_term = high_ref[:, here]
            out_ref[:, there] = dot(high, high_term, NN) + (dot(high, low_ref[:, here], NN) + dot(low, high_term, NN))
            copies.append(pltpu.make_async_copy(out_ref.at[:, there], scores_ref.at[:, there], sems.at[len(copies)]))
            copies[-1].start()
        at += high_ref.shape[1]
    for copy in copies:
        copy.wait()


def solve(me, mine, other, terms):
    order = terms[0].shape[0]
    cells = [term.shape[1] for term in terms[::2]]
    here, square = pl.BlockSpec(memory_space=pltpu.VMEM), (order, order)
    return pl.pallas_call(
        solve_kernel,
        in_specs=[pl.BlockSpec(memory_space=pltpu.SMEM)] + [here] * (2 + len(terms)),
        out_specs=[here, pl.BlockSpec(memory_space=pl.ANY)],
        out_shape=[jax.ShapeDtypeStruct(square, F32), jax.ShapeDtypeStruct((order, sum(cells)), F32)],
        scratch_shapes=[pltpu.VMEM((order, sum(cells)), F32)]
        + [pltpu.VMEM(square, F32)] * 3
        + [pltpu.SemaphoreType.DMA((sum(-(-c // STEP) for c in cells),))],
        compiler_params=pltpu.CompilerParams(vmem_limit_bytes=VMEM_LIMIT),
    )(me[None], mine, other, *terms)


def swap(x, axis, mask):
    return lax.ppermute(x, axis, [(i, i ^ mask) for i in range(lax.axis_size(axis))])


def sum_over(x, axis, first):
    size = lax.axis_size(axis)
    while first < size:
        if 2 * first < size:
            near, far, both = swap(x, axis, first), swap(x, axis, 2 * first), swap(x, axis, 3 * first)
            x = (x + near) + (far + both)
        else:
            x = x + swap(x, axis, first)
        first *= 4
    return x


def on_device(anomaly, ocean_mask, area_weight):
    size = lax.axis_size("dev")
    me = lax.axis_index("dev")
    cells = anomaly.shape[1] // size
    order = sorted(range(1, size), key=lambda k: (-(k >> 1).bit_count(), k & 1))
    sizes = (cells - cells // 4, cells // 4)
    part = lambda k: lax.dynamic_slice_in_dim(anomaly, (me ^ k) * cells, cells, 1)
    pieces = {k: swap(part(k), "dev", k) for k in (order[0], 1)}
    anomaly, pieces[1] = lax.optimization_barrier((anomaly, pieces[1]))
    pieces |= {k: swap(part(k), "dev", k) for k in order if k not in pieces}
    own = lambda x: lax.dynamic_slice_in_dim(x, me * cells, cells, 0)
    weights = own(area_weight) * own(ocean_mask).astype(F32)
    root = jnp.sqrt(weights)[None, :]
    total = jnp.sum(weights)[None, None]
    high, low, keep, send = form_gram(me, part(0), [pieces[k] for k in range(1, size)], root, total)
    mine = keep + swap(send, "dev", 1)
    mine = sum_over(mine, "dev", 2)
    mine = sum_over(mine, "band", 1)
    other = swap(mine, "dev", 1)
    return tuple(solve(me, mine, other, [high, low]))


def solution(mesh):
    return jax.shard_map(
        on_device,
        mesh=mesh,
        in_specs=(P("dev", "band"), P("band"), P("band")),
        out_specs=(P(), P(None, ("band", "dev"))),
        check_vma=False,
    )
```

```python
import functools
import jax
import jax.numpy as jnp
from jax import lax
from jax.experimental import pallas as pl
from jax.experimental.pallas import tpu as pltpu
from jax.sharding import PartitionSpec as P

F32, BF16 = jnp.float32, jnp.bfloat16
SUB, LANE = 8, 128
PANEL = 64
NN = (((1,), (0,)), ((), ()))
NT = (((1,), (1,)), ((), ()))
VMEM_LIMIT = 24 * 1024 * 1024
STEP = 512
RUN = 1024
PARTS = RUN // LANE
KEPT = 3 * RUN // 4
STEPS = (RUN - 1).bit_length()
ALL_VMEM = 62 * 1024 * 1024


def split2(x):
    high = x.astype(BF16)
    return high, (x - high.astype(F32)).astype(BF16)


def split3(x):
    high = x.astype(BF16)
    rest = x - high.astype(F32)
    middle = rest.astype(BF16)
    return high, middle, (rest - middle.astype(F32)).astype(BF16)


def dot(a, b, dims):
    return lax.dot_general(a, b, dims, preferred_element_type=F32)


def product(a, b, dims):
    a1, a2, a3 = a
    b1, b2, b3 = b
    small = (dot(a1, b3, dims) + dot(a3, b1, dims)) + dot(a2, b2, dims)
    return dot(a1, b1, dims) + ((dot(a1, b2, dims) + dot(a2, b1, dims)) + small)


def tree_sum(terms):
    while len(terms) > 1:
        terms = [sum(terms[i : i + 2][1:], terms[i]) for i in range(0, len(terms), 2)]
    return terms[0]


def row_of(x, k):
    return jnp.broadcast_to(x[k : k + 1, :], (SUB, LANE))


def column_of(x, k):
    return jnp.broadcast_to(x[:, k : k + 1], (SUB, LANE))


def factor_panel(tiles, start):
    tiles = list(tiles)
    count = len(tiles)
    sub = lax.broadcasted_iota(jnp.int32, (SUB, LANE), 0)
    diag = [column_of(tiles[0], start + k) for k in range(SUB)]
    for b in range(count):
        rest = range(b + 1, count)
        cols = {t: [column_of(tiles[t], start + SUB * b + k) for k in range(SUB)] for t in rest}
        ahead = [column_of(tiles[b + 1], start + SUB * (b + 1) + k) for k in range(SUB)] if b + 1 < count else None
        rows = []
        for j in range(SUB):
            inverse = lax.rsqrt(row_of(diag[j], j))
            own = diag[j] * inverse
            spread = {k: row_of(own, k) for k in range(j + 1, SUB)}
            for k in range(j + 1, SUB):
                diag[k] = diag[k] - own * spread[k]
            for t in rest:
                cols[t][j] = cols[t][j] * inverse
                for k in range(j + 1, SUB):
                    cols[t][k] = cols[t][k] - cols[t][j] * spread[k]
            row = row_of(tiles[b], j) * inverse
            tiles[b] = jnp.where(sub == j, row, jnp.where(sub > j, tiles[b] - own * row, tiles[b]))
            rows.append(row)
        if ahead is not None:
            below = cols[b + 1]
            diag = [ahead[k] - tree_sum([below[j] * row_of(below[j], k) for j in range(SUB)]) for k in range(SUB)]
        for t in rest:
            tiles[t] = tiles[t] - tree_sum([cols[t][j] * rows[j] for j in range(SUB)])
    return tiles


def cholesky_and_inverse(a_ref, inverse_ref, upper_ref, lower_ref):
    order = a_ref.shape[0]
    inverse_ref[...] = jnp.zeros((order, order), F32)
    upper_ref[...] = jnp.zeros((order, order), F32)
    lane = lax.broadcasted_iota(jnp.int32, (SUB, PANEL), 1)
    sub = lax.broadcasted_iota(jnp.int32, (SUB, PANEL), 0)
    block_row = lax.broadcasted_iota(jnp.int32, (PANEL, PANEL), 0)
    block_col = lax.broadcasted_iota(jnp.int32, (PANEL, PANEL), 1)
    for first in range(0, order, PANEL):
        end = first + PANEL
        column = a_ref[first:, first:end]
        if first:
            done = split3(lower_ref[first:, :first])
            column = column - product(done, tuple(term[:PANEL] for term in done), NT)
        tiles = []
        for t in range(PANEL // SUB):
            eye = jnp.where(lane == sub + SUB * t, 1.0, 0.0)
            tiles.append(jnp.concatenate([column[SUB * t : SUB * t + SUB], eye], 1))
        both = jnp.concatenate(factor_panel(tiles, 0), 0)
        upper_ref[first:end, first:end] = jnp.where(block_col >= block_row, both[:, :PANEL], 0.0)
        own = both[:, PANEL:]
        own_terms = split3(own)
        if end < order:
            lower = product(split3(column[PANEL:]), own_terms, NT)
            lower_ref[end:, first:end] = lower
            upper_ref[first:end, end:] = lower.T
        if first:
            behind = product(tuple(term[:PANEL] for term in done), split3(inverse_ref[:first, :first]), NN)
            inverse_ref[first:end, :first] = -product(own_terms, split3(behind), NN)
        inverse_ref[first:end, first:end] = own


HERE = pl.BlockSpec(memory_space=pltpu.VMEM)
SCALARS = pl.BlockSpec(memory_space=pltpu.SMEM)


def call(kernel, operands, outs, scratch=(), scalars=1, us=1):
    return pl.pallas_call(
        kernel,
        in_specs=[SCALARS] * scalars + [HERE] * (len(operands) - scalars),
        out_specs=[HERE] * len(outs),
        out_shape=outs,
        scratch_shapes=scratch,
        compiler_params=pltpu.CompilerParams(vmem_limit_bytes=VMEM_LIMIT),
        cost_estimate=pl.CostEstimate(flops=us * 1_000_000_000, bytes_accessed=us * 3_600_000, transcendentals=0),
    )(*operands)


def shift_left(parts, by):
    if by >= LANE:
        return parts[by // LANE :] + [jnp.zeros_like(parts[0])] * (by // LANE)
    lane = lax.broadcasted_iota(jnp.int32, parts[0].shape, 1)
    turned = [pltpu.roll(part, LANE - by, 1) for part in parts] + [jnp.zeros_like(parts[0])]
    return [jnp.where(lane < LANE - by, here, after) for here, after in zip(turned, turned[1:])]


def plan(mask_ref, source_ref, rank_ref, over_ref, gap_ref):
    groups = mask_ref.shape[0]
    runs = groups // PARTS
    chunk = min(groups, 2 * LANE)
    bit = lambda keep: jnp.where(keep, 1.0, 0.0).astype(BF16)
    iota = lambda shape, axis: lax.broadcasted_iota(jnp.int32, shape, axis)
    before = bit(iota((LANE, LANE), 0) < iota((LANE, LANE), 1))
    row, col = iota((chunk, chunk), 0), iota((chunk, chunk), 1)
    earlier = bit((row // PARTS == col // PARTS) & (col < row))
    for first in range(0, groups, chunk):
        mask = mask_ref[first : first + chunk, :]
        land = (1 - mask).astype(F32).astype(BF16)
        carried = dot(dot(earlier, land, NN).astype(BF16), jnp.ones((LANE, LANE), BF16), NN)
        gap_ref[first : first + chunk, :] = (dot(land, before, NN) + carried).astype(jnp.int32)
    mask = [mask_ref[pl.ds(p, runs, stride=PARTS), :] for p in range(PARTS)]
    gap = [gap_ref[pl.ds(p, runs, stride=PARTS), :] for p in range(PARTS)]
    last = gap[-1] + (1 - mask[-1])
    count = RUN - jnp.broadcast_to(last[:, LANE - 1 :], (runs, LANE))
    over_ref[...] = jnp.broadcast_to(jnp.max(jnp.where(count > KEPT, 1.0, 0.0), axis=0, keepdims=True), (SUB, LANE))
    lane = iota((runs, LANE), 1)
    for p in range(PARTS):
        rank_ref[p] = jnp.where(mask[p] != 0, lane + p * LANE - gap[p], -1)
    gap = [g * m for g, m in zip(gap, mask)]
    for step in range(STEPS):
        moved = [jnp.where((g & (1 << step)) != 0, g, 0) for g in gap]
        gap = [g - m + a for g, m, a in zip(gap, moved, shift_left(moved, 1 << step))]
    for p in range(PARTS):
        at = lane + p * LANE
        source_ref[p] = jnp.where(at < count, at + gap[p], -1)


def across(ref, at, run):
    return jnp.broadcast_to(ref[at, pl.ds(run, 1), :], (SUB, LANE))


def gathered(parts, index):
    lane, part = index & (LANE - 1), index >> (LANE.bit_length() - 1)
    out = jnp.zeros((SUB, LANE), F32)
    for p, x in parts.items():
        out = jnp.where(part == p, jnp.take_along_axis(x, lane, axis=1, mode="promise_in_bounds"), out)
    return out


def pack(to, x_ref, root_ref, source_ref, out_ref, first):
    rows, cells = x_ref.shape
    runs = cells // RUN
    width = out_ref.shape[1] // runs
    for run in range(runs):
        places = range(first // LANE, (first + width) // LANE)
        index = {p: across(source_ref, p, to * runs + run) for p in places}
        for t in range(0, rows, SUB):
            parts = []
            for group in range(run * PARTS, (run + 1) * PARTS):
                root = jnp.broadcast_to(root_ref[group : group + 1, :], (SUB, LANE))
                parts.append(x_ref[t : t + SUB, group * LANE : (group + 1) * LANE] * root)
            for p in places:
                at = run * width + p * LANE - first
                out_ref[t : t + SUB, at : at + LANE] = gathered({i: parts[i] for i in range(p, PARTS)}, index[p])


def slice_copies(to, x_ref, area_ref, own_ref, own_area_ref, sems):
    cells = own_ref.shape[1]
    groups = cells // LANE
    return [
        pltpu.make_async_copy(area_ref.at[pl.ds(pl.multiple_of(to * groups, groups), groups), :], own_area_ref, sems.at[0]),
        pltpu.make_async_copy(x_ref.at[:, pl.ds(pl.multiple_of(to * cells, cells), cells)], own_ref, sems.at[1]),
    ]


def first_kernel(to_ref, x_ref, mask_ref, area_ref, source_ref, rank_ref, over_ref, kept_ref, *scratch):
    own_ref, own_area_ref, root_ref, whole_mask_ref, gap_ref, sems = scratch
    groups = own_area_ref.shape[0]
    to = to_ref[0]
    mask_copy = pltpu.make_async_copy(mask_ref, whole_mask_ref, sems.at[2])
    mask_copy.start()
    copies = slice_copies(to, x_ref, area_ref, own_ref, own_area_ref, sems)
    for copy in copies:
        copy.start()
    mask_copy.wait()
    plan(whole_mask_ref, source_ref, rank_ref, over_ref, gap_ref)
    for copy in copies:
        copy.wait()
    mask = whole_mask_ref[pl.ds(pl.multiple_of(to * groups, groups), groups), :]
    root_ref[...] = jnp.sqrt(own_area_ref[...] * mask.astype(F32))
    pack(to, own_ref, root_ref, source_ref, kept_ref, 0)


def second_kernel(to_ref, x_ref, mask_ref, area_ref, source_ref, gate_ref, kept_ref, *scratch):
    own_ref, own_area_ref, root_ref, own_mask_ref, sems = scratch
    groups = own_area_ref.shape[0]
    to = to_ref[0]
    at = pl.ds(pl.multiple_of(to * groups, groups), groups)
    copies = slice_copies(to, x_ref, area_ref, own_ref, own_area_ref, sems)
    copies.append(pltpu.make_async_copy(mask_ref.at[at, :], own_mask_ref, sems.at[2]))
    for copy in copies:
        copy.start()
    for copy in copies:
        copy.wait()
    root_ref[...] = jnp.sqrt(own_area_ref[...] * own_mask_ref[...].astype(F32))
    pack(to, own_ref, root_ref, source_ref, kept_ref, 0)


def pack_early(to, anomaly, mask, area, cells, source=None, gate=None):
    rows, groups, own_groups = anomaly.shape[0], mask.shape[0], cells // LANE
    moves = jax.ShapeDtypeStruct((PARTS, groups // PARTS, LANE), jnp.int32)
    outs = [jax.ShapeDtypeStruct((rows, cells // RUN * KEPT), F32)]
    scratch = [pltpu.VMEM((rows, cells), F32)] + [pltpu.VMEM((own_groups, LANE), F32)] * 2
    operands, specs = [to[None], anomaly, mask, area], [SCALARS] + [pl.BlockSpec(memory_space=pl.ANY)] * 3
    if source is None:
        kernel = first_kernel
        outs = [moves, moves, jax.ShapeDtypeStruct((SUB, LANE), F32)] + outs
        scratch += [pltpu.VMEM((groups, LANE), jnp.int32)] * 2
    else:
        kernel = second_kernel
        operands, specs = operands + [source, gate], specs + [HERE] * 2
        scratch += [pltpu.VMEM((own_groups, LANE), jnp.int32)]
    return pl.pallas_call(
        kernel,
        in_specs=specs,
        out_specs=[HERE] * len(outs),
        out_shape=outs,
        scratch_shapes=scratch + [pltpu.SemaphoreType.DMA((3,))],
        compiler_params=pltpu.CompilerParams(vmem_limit_bytes=ALL_VMEM),
        cost_estimate=pl.CostEstimate(flops=2_000_000_000, bytes_accessed=7_200_000, transcendentals=0),
    )(*operands)


def pack_kernel(first, to_ref, x_ref, mask_ref, area_ref, source_ref, out_ref, root_ref):
    groups = x_ref.shape[1] // LANE
    to = to_ref[0]
    at = pl.ds(pl.multiple_of(to * groups, groups), groups)
    root_ref[...] = jnp.sqrt(area_ref[at, :] * mask_ref[at, :].astype(F32))
    pack(to, x_ref, root_ref, source_ref, out_ref, first)


def pack_cells(to, x, mask, area, source, rest=False):
    rows, cells = x.shape
    out = jax.ShapeDtypeStruct((rows, cells // RUN * (RUN - KEPT if rest else KEPT)), F32)
    kernel = functools.partial(pack_kernel, KEPT if rest else 0)
    return call(kernel, [to[None], x, mask, area, source], [out], [pltpu.VMEM((cells // LANE, LANE), F32)])[0]


def spread_kernel(me_ref, rank_ref, kept_ref, *refs):
    out_ref = refs[-1]
    rows, cells = out_ref.shape
    runs = cells // RUN
    me = me_ref[0]
    for run in range(runs):
        index = [across(rank_ref, p, me * runs + run) for p in range(PARTS)]
        for t in range(0, rows, SUB):
            parts = [kept_ref[t : t + SUB, first : first + LANE] for first in range(run * KEPT, (run + 1) * KEPT, LANE)]
            for ref in refs[:-1]:
                width = RUN - KEPT
                parts += [ref[t : t + SUB, first : first + LANE] for first in range(run * width, (run + 1) * width, LANE)]
            for p in range(PARTS):
                first = run * RUN + p * LANE
                out_ref[t : t + SUB, first : first + LANE] = gathered({i: parts[i] for i in range(min(p + 1, len(parts)))}, index[p])


def spread(me, rank, kept, *rest):
    out = jax.ShapeDtypeStruct((kept.shape[0], kept.shape[1] // KEPT * RUN), F32)
    return call(spread_kernel, [me[None], rank, kept, *rest], [out])[0]


def place(me, refs, at, whole_ref):
    rows = refs[0].shape[0]
    for k, ref in enumerate(refs):
        whole_ref[pl.ds(pl.multiple_of((me ^ k) * rows, rows), rows), at] = ref[:, at]


def products(me, piece_refs, whole_ref):
    main = cross = None
    cells = piece_refs[0].shape[1]
    for first in range(0, cells, STEP):
        at = slice(first, min(first + STEP, cells))
        place(me, piece_refs, at, whole_ref)
        high, low = split2(whole_ref[:, at])
        more_main, more_cross = dot(high, high, NT), dot(high, low, NT)
        main, cross = (main + more_main, cross + more_cross) if first else (more_main, more_cross)
    return main + (cross + cross.T)


def gram_kernel(pieces, me_ref, *refs):
    piece_refs, (total_ref, over_ref, keep_ref, send_ref, whole_ref, sum_ref) = refs[:pieces], refs[pieces:]
    me = me_ref[0]
    sum_ref[...] = products(me, piece_refs, whole_ref)
    half = sum_ref.shape[0] // 2
    row = lax.broadcasted_iota(jnp.int32, (half, half), 0)
    col = lax.broadcasted_iota(jnp.int32, (half, half), 1)
    last = sum_ref[half:, half:]
    both = jnp.where(row >= col, sum_ref[:half, :half], last)
    corner = jnp.sum(jnp.where(row == col, last, 0.0), axis=0, keepdims=True)
    extra_row = lax.broadcasted_iota(jnp.int32, (SUB, half), 0)
    extra = jnp.where(extra_row == 0, jnp.broadcast_to(corner, (SUB, half)), jnp.broadcast_to(total_ref[...], (SUB, half)))
    extra = jnp.where(extra_row == SUB - 1, jnp.broadcast_to(over_ref[:1, :1], (SUB, half)), extra)
    off = sum_ref[half:, :half]
    first_core = (me & 1) == 0
    for ref, is_off in ((keep_ref, first_core), (send_ref, jnp.logical_not(first_core))):
        ref[:half, :] = jnp.where(is_off, off, both)
        ref[half:, :] = extra


def form_gram(me, pieces, total, over):
    rows, cells = pieces[0].shape
    order = rows * len(pieces)
    packed = jax.ShapeDtypeStruct((order // 2 + SUB, order // 2), F32)
    scratch = [pltpu.VMEM((order, cells), F32), pltpu.VMEM((order, order), F32)]
    return call(functools.partial(gram_kernel, len(pieces)), [me[None], *pieces, total, over], [packed] * 2, scratch, us=2)


def terms_kernel(pieces, me_ref, *refs):
    piece_refs, (high_ref, low_ref, whole_ref) = refs[:pieces], refs[pieces:]
    place(me_ref[0], piece_refs, slice(None), whole_ref)
    high_ref[...], low_ref[...] = split2(whole_ref[...])


def form_terms(me, pieces):
    rows, cells = pieces[0].shape
    out = jax.ShapeDtypeStruct((rows * len(pieces), cells), BF16)
    scratch = [pltpu.VMEM(out.shape, F32)]
    return call(functools.partial(terms_kernel, len(pieces)), [me[None], *pieces], [out] * 2, scratch)


def solve_kernel(me_ref, mine_ref, other_ref, *refs):
    term_refs, (upper_ref, scores_ref, out_ref, a_ref, inverse_ref, lower_ref, sems) = refs[:-7], refs[-7:]
    half = mine_ref.shape[1]
    first_core = (me_ref[0] & 1) == 0
    mine, other = mine_ref[...], other_ref[...]
    off = jnp.where(first_core, mine[:half], other[:half])
    both = jnp.where(first_core, other[:half], mine[:half])
    scale = 1.0 / mine[half + 1 : half + 2, :]
    row = lax.broadcasted_iota(jnp.int32, (half, half), 0)
    col = lax.broadcasted_iota(jnp.int32, (half, half), 1)
    turned = both.T
    corner = jnp.broadcast_to(mine[half : half + 1, :], (half, half))
    a_ref[:half, :half] = jnp.where(row >= col, both, turned) * scale
    a_ref[half:, half:] = jnp.where(row < col, both, jnp.where(row > col, turned, corner)) * scale
    a_ref[half:, :half] = off * scale
    cholesky_and_inverse(a_ref, inverse_ref, upper_ref, lower_ref)
    high, low = split2(inverse_ref[...])
    copies, at = [], 0
    for high_ref, low_ref in zip(term_refs[::2], term_refs[1::2]):
        for first in range(0, high_ref.shape[1], STEP):
            here = slice(first, min(first + STEP, high_ref.shape[1]))
            there = slice(at + here.start, at + here.stop)
            high_term = high_ref[:, here]
            out_ref[:, there] = dot(high, high_term, NN) + (dot(high, low_ref[:, here], NN) + dot(low, high_term, NN))
            copies.append(pltpu.make_async_copy(out_ref.at[:, there], scores_ref.at[:, there], sems.at[len(copies)]))
            copies[-1].start()
        at += high_ref.shape[1]
    for copy in copies:
        copy.wait()


def solve(me, mine, other, terms):
    order = terms[0].shape[0]
    cells = [term.shape[1] for term in terms[::2]]
    here, square = pl.BlockSpec(memory_space=pltpu.VMEM), (order, order)
    return pl.pallas_call(
        solve_kernel,
        in_specs=[pl.BlockSpec(memory_space=pltpu.SMEM)] + [here] * (2 + len(terms)),
        out_specs=[here, pl.BlockSpec(memory_space=pl.ANY)],
        out_shape=[jax.ShapeDtypeStruct(square, F32), jax.ShapeDtypeStruct((order, sum(cells)), F32)],
        scratch_shapes=[pltpu.VMEM((order, sum(cells)), F32)]
        + [pltpu.VMEM(square, F32)] * 3
        + [pltpu.SemaphoreType.DMA((sum(-(-c // STEP) for c in cells),))],
        compiler_params=pltpu.CompilerParams(vmem_limit_bytes=VMEM_LIMIT),
    )(me[None], mine, other, *terms)


def swap(x, axis, mask):
    return lax.ppermute(x, axis, [(i, i ^ mask) for i in range(lax.axis_size(axis))])


def reduce_over(op, x, axis, first):
    size = lax.axis_size(axis)
    while first < size:
        if 2 * first < size:
            near, far, both = swap(x, axis, first), swap(x, axis, 2 * first), swap(x, axis, 3 * first)
            x = op(op(x, near), op(far, both))
        else:
            x = op(x, swap(x, axis, first))
        first *= 4
    return x


def sum_all(keep, send):
    mine = keep + swap(send, "dev", 1)
    mine = reduce_over(jnp.add, mine, "dev", 2)
    mine = reduce_over(jnp.add, mine, "band", 1)
    return mine, swap(mine, "dev", 1)


def on_device(anomaly, ocean_mask, area_weight):
    size = lax.axis_size("dev")
    me = lax.axis_index("dev")
    cells = anomaly.shape[1] // size
    order = sorted(range(1, size), key=lambda k: (-(k >> 1).bit_count(), k & 1))
    mask, area = ocean_mask.reshape(-1, LANE), area_weight.reshape(-1, LANE)
    others, every = range(1, size), range(size)
    part = lambda k: lax.dynamic_slice_in_dim(anomaly, (me ^ k) * cells, cells, 1)
    kept = {}
    source, rank, over, packed = pack_early(me ^ order[0], anomaly, mask, area, cells)
    kept[order[0]] = swap(packed, "dev", order[0])
    if size > 2:
        packed = pack_early(me ^ order[1], anomaly, mask, area, cells, source, swap(over, "dev", 1))[0]
        kept[order[1]] = swap(packed, "dev", order[1])
        anomaly, source, packed = lax.optimization_barrier((anomaly, source, packed))
    for k in (*order[2:], 0):
        packed = pack_cells(me ^ k, part(k), mask, area, source)
        kept[k] = swap(packed, "dev", k) if k else packed
    cut = lambda x: lax.dynamic_slice_in_dim(x, me * cells, cells, 0)
    weights = cut(area_weight) * cut(ocean_mask).astype(F32)
    total = jnp.sum(weights)[None, None]
    scaled = part(0) * jnp.sqrt(weights)[None, :]
    late = order[-3:-1]
    pieces = {k: spread(me, rank, kept[k]) for k in others if k not in late}
    pieces[0] = scaled
    last = kept[late[-1]] if late else kept[1]
    last, pieces = lax.optimization_barrier((last, pieces))
    if late:
        kept[late[-1]] = last
    kept = [kept[k] for k in every]
    keep, send = form_gram(me, kept, total, over)
    mine = keep + swap(send, "dev", 1)
    for k, axis, first in zip(late, ("dev", "band"), (2, 1)):
        mine, rank = lax.optimization_barrier((mine, rank))
        pieces[k] = spread(me, rank, kept[k])
        mine = reduce_over(jnp.add, mine, axis, first)
    terms = form_terms(me, [pieces[k] for k in every])
    mine, terms = lax.optimization_barrier((mine, terms))
    other = swap(mine, "dev", 1)
    flag = mine[-1, 0] > 0

    def all_sent(mine, other):
        return solve(me, mine, other, terms)

    def send_rest(mine, other):
        rest = [pack_cells(me ^ k, part(k), mask, area, source, True) for k in every]
        rest = rest[:1] + [swap(x, "dev", k) for k, x in zip(others, rest[1:])]
        more_mine, more_other = sum_all(*form_gram(me, rest, jnp.zeros_like(total), over))
        pieces = [scaled] + [spread(me, rank, kept[k], rest[k]) for k in others]
        return solve(me, mine + more_mine, other + more_other, form_terms(me, pieces))

    return tuple(lax.cond(flag, send_rest, all_sent, mine, other))


def solution(mesh):
    return jax.shard_map(
        on_device,
        mesh=mesh,
        in_specs=(P("dev", "band"), P("band"), P("band")),
        out_specs=(P(), P(None, ("band", "dev"))),
        check_vma=False,
    )
```

```python
import functools
import jax
import jax.numpy as jnp
from jax import lax
from jax.experimental import pallas as pl
from jax.experimental.pallas import tpu as pltpu
from jax.sharding import PartitionSpec as P

F32, BF16 = jnp.float32, jnp.bfloat16
SUB, LANE = 8, 128
PANEL = 64
NN = (((1,), (0,)), ((), ()))
NT = (((1,), (1,)), ((), ()))
VMEM_LIMIT = 24 * 1024 * 1024
STEP = 512
RUN = 1024
PARTS = RUN // LANE
KEPT = 3 * RUN // 4
STEPS = (RUN - 1).bit_length()


def split2(x):
    high = x.astype(BF16)
    return high, (x - high.astype(F32)).astype(BF16)


def split3(x):
    high = x.astype(BF16)
    rest = x - high.astype(F32)
    middle = rest.astype(BF16)
    return high, middle, (rest - middle.astype(F32)).astype(BF16)


def dot(a, b, dims):
    return lax.dot_general(a, b, dims, preferred_element_type=F32)


def product(a, b, dims):
    a1, a2, a3 = a
    b1, b2, b3 = b
    small = (dot(a1, b3, dims) + dot(a3, b1, dims)) + dot(a2, b2, dims)
    return dot(a1, b1, dims) + ((dot(a1, b2, dims) + dot(a2, b1, dims)) + small)


def tree_sum(terms):
    while len(terms) > 1:
        terms = [sum(terms[i : i + 2][1:], terms[i]) for i in range(0, len(terms), 2)]
    return terms[0]


def row_of(x, k):
    return jnp.broadcast_to(x[k : k + 1, :], (SUB, LANE))


def column_of(x, k):
    return jnp.broadcast_to(x[:, k : k + 1], (SUB, LANE))


def factor_panel(tiles, start):
    tiles = list(tiles)
    count = len(tiles)
    sub = lax.broadcasted_iota(jnp.int32, (SUB, LANE), 0)
    diag = [column_of(tiles[0], start + k) for k in range(SUB)]
    for b in range(count):
        rest = range(b + 1, count)
        cols = {t: [column_of(tiles[t], start + SUB * b + k) for k in range(SUB)] for t in rest}
        ahead = [column_of(tiles[b + 1], start + SUB * (b + 1) + k) for k in range(SUB)] if b + 1 < count else None
        rows = []
        for j in range(SUB):
            inverse = lax.rsqrt(row_of(diag[j], j))
            own = diag[j] * inverse
            spread = {k: row_of(own, k) for k in range(j + 1, SUB)}
            for k in range(j + 1, SUB):
                diag[k] = diag[k] - own * spread[k]
            for t in rest:
                cols[t][j] = cols[t][j] * inverse
                for k in range(j + 1, SUB):
                    cols[t][k] = cols[t][k] - cols[t][j] * spread[k]
            row = row_of(tiles[b], j) * inverse
            tiles[b] = jnp.where(sub == j, row, jnp.where(sub > j, tiles[b] - own * row, tiles[b]))
            rows.append(row)
        if ahead is not None:
            below = cols[b + 1]
            diag = [ahead[k] - tree_sum([below[j] * row_of(below[j], k) for j in range(SUB)]) for k in range(SUB)]
        for t in rest:
            tiles[t] = tiles[t] - tree_sum([cols[t][j] * rows[j] for j in range(SUB)])
    return tiles


def cholesky_and_inverse(a_ref, inverse_ref, upper_ref, lower_ref):
    order = a_ref.shape[0]
    inverse_ref[...] = jnp.zeros((order, order), F32)
    upper_ref[...] = jnp.zeros((order, order), F32)
    lane = lax.broadcasted_iota(jnp.int32, (SUB, PANEL), 1)
    sub = lax.broadcasted_iota(jnp.int32, (SUB, PANEL), 0)
    block_row = lax.broadcasted_iota(jnp.int32, (PANEL, PANEL), 0)
    block_col = lax.broadcasted_iota(jnp.int32, (PANEL, PANEL), 1)
    for first in range(0, order, PANEL):
        end = first + PANEL
        column = a_ref[first:, first:end]
        if first:
            done = split3(lower_ref[first:, :first])
            column = column - product(done, tuple(term[:PANEL] for term in done), NT)
        tiles = []
        for t in range(PANEL // SUB):
            eye = jnp.where(lane == sub + SUB * t, 1.0, 0.0)
            tiles.append(jnp.concatenate([column[SUB * t : SUB * t + SUB], eye], 1))
        both = jnp.concatenate(factor_panel(tiles, 0), 0)
        upper_ref[first:end, first:end] = jnp.where(block_col >= block_row, both[:, :PANEL], 0.0)
        own = both[:, PANEL:]
        own_terms = split3(own)
        if end < order:
            lower = product(split3(column[PANEL:]), own_terms, NT)
            lower_ref[end:, first:end] = lower
            upper_ref[first:end, end:] = lower.T
        if first:
            behind = product(tuple(term[:PANEL] for term in done), split3(inverse_ref[:first, :first]), NN)
            inverse_ref[first:end, :first] = -product(own_terms, split3(behind), NN)
        inverse_ref[first:end, first:end] = own


HERE = pl.BlockSpec(memory_space=pltpu.VMEM)
SCALARS = pl.BlockSpec(memory_space=pltpu.SMEM)


def call(kernel, operands, outs, scratch=(), scalars=1, us=1):
    return pl.pallas_call(
        kernel,
        in_specs=[SCALARS] * scalars + [HERE] * (len(operands) - scalars),
        out_specs=[HERE] * len(outs),
        out_shape=outs,
        scratch_shapes=scratch,
        compiler_params=pltpu.CompilerParams(vmem_limit_bytes=VMEM_LIMIT),
        cost_estimate=pl.CostEstimate(flops=us * 1_000_000_000, bytes_accessed=us * 3_600_000, transcendentals=0),
    )(*operands)


def shift_left(parts, by):
    if by >= LANE:
        return parts[by // LANE :] + [jnp.zeros_like(parts[0])] * (by // LANE)
    lane = lax.broadcasted_iota(jnp.int32, parts[0].shape, 1)
    turned = [pltpu.roll(part, LANE - by, 1) for part in parts] + [jnp.zeros_like(parts[0])]
    return [jnp.where(lane < LANE - by, here, after) for here, after in zip(turned, turned[1:])]


def plan(mask_ref, source_ref, rank_ref, over_ref, gap_ref):
    groups = mask_ref.shape[0]
    runs = groups // PARTS
    chunk = min(groups, 2 * LANE)
    bit = lambda keep: jnp.where(keep, 1.0, 0.0).astype(BF16)
    iota = lambda shape, axis: lax.broadcasted_iota(jnp.int32, shape, axis)
    before = bit(iota((LANE, LANE), 0) < iota((LANE, LANE), 1))
    row, col = iota((chunk, chunk), 0), iota((chunk, chunk), 1)
    earlier = bit((row // PARTS == col // PARTS) & (col < row))
    for first in range(0, groups, chunk):
        mask = mask_ref[first : first + chunk, :]
        land = (1 - mask).astype(F32).astype(BF16)
        carried = dot(dot(earlier, land, NN).astype(BF16), jnp.ones((LANE, LANE), BF16), NN)
        gap_ref[first : first + chunk, :] = (dot(land, before, NN) + carried).astype(jnp.int32)
    mask = [mask_ref[pl.ds(p, runs, stride=PARTS), :] for p in range(PARTS)]
    gap = [gap_ref[pl.ds(p, runs, stride=PARTS), :] for p in range(PARTS)]
    last = gap[-1] + (1 - mask[-1])
    count = RUN - jnp.broadcast_to(last[:, LANE - 1 :], (runs, LANE))
    over_ref[...] = jnp.broadcast_to(jnp.max(jnp.where(count > KEPT, 1.0, 0.0), axis=0, keepdims=True), (SUB, LANE))
    lane = iota((runs, LANE), 1)
    for p in range(PARTS):
        rank_ref[p] = jnp.where(mask[p] != 0, lane + p * LANE - gap[p], -1)
    gap = [g * m for g, m in zip(gap, mask)]
    for step in range(STEPS):
        moved = [jnp.where((g & (1 << step)) != 0, g, 0) for g in gap]
        gap = [g - m + a for g, m, a in zip(gap, moved, shift_left(moved, 1 << step))]
    for p in range(PARTS):
        at = lane + p * LANE
        source_ref[p] = jnp.where(at < count, at + gap[p], -1)


def across(ref, at, run):
    return jnp.broadcast_to(ref[at, pl.ds(run, 1), :], (SUB, LANE))


def gathered(parts, index):
    lane, part = index & (LANE - 1), index >> (LANE.bit_length() - 1)
    out = jnp.zeros((SUB, LANE), F32)
    for p, x in parts.items():
        out = jnp.where(part == p, jnp.take_along_axis(x, lane, axis=1, mode="promise_in_bounds"), out)
    return out


def pack(base, x_ref, root_ref, source_ref, out_ref):
    rows, cells = x_ref.shape
    for run in range(cells // RUN):
        index = [across(source_ref, p, base + run) for p in range(KEPT // LANE)]
        for t in range(0, rows, SUB):
            parts = []
            for group in range(run * PARTS, (run + 1) * PARTS):
                root = jnp.broadcast_to(root_ref[group : group + 1, :], (SUB, LANE))
                parts.append(x_ref[t : t + SUB, group * LANE : (group + 1) * LANE] * root)
            for p, lanes in enumerate(index):
                at = run * KEPT + p * LANE
                out_ref[t : t + SUB, at : at + LANE] = gathered({i: parts[i] for i in range(p, PARTS)}, lanes)


def groups_from(base, groups):
    return pl.ds(pl.multiple_of(base * PARTS, PARTS), groups)


def first_kernel(base_ref, x_ref, mask_ref, area_ref, gate_ref, source_ref, rank_ref, over_ref, out_ref, root_ref, gap_ref):
    base = base_ref[0]
    plan(mask_ref, source_ref, rank_ref, over_ref, gap_ref)
    at = groups_from(base, root_ref.shape[0])
    root_ref[...] = jnp.sqrt(area_ref[at, :] * mask_ref[at, :].astype(F32))
    pack(base, x_ref, root_ref, source_ref, out_ref)


def plan_and_pack(base, x, mask, area, gate):
    rows, cells = x.shape
    groups = mask.shape[0]
    moves = jax.ShapeDtypeStruct((PARTS, groups // PARTS, LANE), jnp.int32)
    outs = [moves, moves, jax.ShapeDtypeStruct((SUB, LANE), F32), jax.ShapeDtypeStruct((rows, cells // RUN * KEPT), F32)]
    scratch = [pltpu.VMEM((cells // LANE, LANE), F32), pltpu.VMEM((groups, LANE), jnp.int32)]
    return call(first_kernel, [base[None], x, mask, area, gate], outs, scratch, us=2)


def pack_kernel(base_ref, x_ref, mask_ref, area_ref, source_ref, *refs):
    out_ref, root_ref = refs[-2:]
    base = base_ref[0]
    at = groups_from(base, root_ref.shape[0])
    root_ref[...] = jnp.sqrt(area_ref[at, :] * mask_ref[at, :].astype(F32))
    pack(base, x_ref, root_ref, source_ref, out_ref)


def pack_cells(base, x, mask, area, source, *gate):
    rows, cells = x.shape
    out = jax.ShapeDtypeStruct((rows, cells // RUN * KEPT), F32)
    return call(pack_kernel, [base[None], x, mask, area, source, *gate], [out], [pltpu.VMEM((cells // LANE, LANE), F32)])[0]


def spread_kernel(me_ref, rank_ref, kept_ref, out_ref):
    rows, cells = out_ref.shape
    runs = cells // RUN
    for run in range(runs):
        index = [across(rank_ref, p, me_ref[0] * runs + run) for p in range(PARTS)]
        for t in range(0, rows, SUB):
            parts = [kept_ref[t : t + SUB, first : first + LANE] for first in range(run * KEPT, (run + 1) * KEPT, LANE)]
            for p in range(PARTS):
                first = run * RUN + p * LANE
                out_ref[t : t + SUB, first : first + LANE] = gathered({i: parts[i] for i in range(min(p + 1, len(parts)))}, index[p])


def spread(me, rank, kept):
    out = jax.ShapeDtypeStruct((kept.shape[0], kept.shape[1] // KEPT * RUN), F32)
    return call(spread_kernel, [me[None], rank, kept], [out])[0]


def place(me, refs, at, whole_ref):
    rows = refs[0].shape[0]
    for k, ref in enumerate(refs):
        whole_ref[pl.ds(pl.multiple_of((me ^ k) * rows, rows), rows), at] = ref[:, at]


def products(me, piece_refs, whole_ref):
    main = cross = None
    cells = piece_refs[0].shape[1]
    for first in range(0, cells, STEP):
        at = slice(first, min(first + STEP, cells))
        place(me, piece_refs, at, whole_ref)
        high, low = split2(whole_ref[:, at])
        more_main, more_cross = dot(high, high, NT), dot(high, low, NT)
        main, cross = (main + more_main, cross + more_cross) if first else (more_main, more_cross)
    return main + (cross + cross.T)


def gram_kernel(pieces, me_ref, *refs):
    piece_refs, (total_ref, over_ref, keep_ref, send_ref, whole_ref, sum_ref) = refs[:pieces], refs[pieces:]
    me = me_ref[0]
    sum_ref[...] = products(me, piece_refs, whole_ref)
    half = sum_ref.shape[0] // 2
    row = lax.broadcasted_iota(jnp.int32, (half, half), 0)
    col = lax.broadcasted_iota(jnp.int32, (half, half), 1)
    last = sum_ref[half:, half:]
    both = jnp.where(row >= col, sum_ref[:half, :half], last)
    corner = jnp.sum(jnp.where(row == col, last, 0.0), axis=0, keepdims=True)
    extra_row = lax.broadcasted_iota(jnp.int32, (SUB, half), 0)
    extra = jnp.where(extra_row == 0, jnp.broadcast_to(corner, (SUB, half)), jnp.broadcast_to(total_ref[...], (SUB, half)))
    extra = jnp.where(extra_row == SUB - 1, jnp.broadcast_to(over_ref[:1, :1], (SUB, half)), extra)
    off = sum_ref[half:, :half]
    first_core = (me & 1) == 0
    for ref, is_off in ((keep_ref, first_core), (send_ref, jnp.logical_not(first_core))):
        ref[:half, :] = jnp.where(is_off, off, both)
        ref[half:, :] = extra


def form_gram(me, pieces, total, over):
    rows, cells = pieces[0].shape
    order = rows * len(pieces)
    packed = jax.ShapeDtypeStruct((order // 2 + SUB, order // 2), F32)
    scratch = [pltpu.VMEM((order, cells), F32), pltpu.VMEM((order, order), F32)]
    return call(functools.partial(gram_kernel, len(pieces)), [me[None], *pieces, total, over], [packed] * 2, scratch, us=2)


def terms_kernel(pieces, me_ref, *refs):
    piece_refs, (high_ref, low_ref, whole_ref) = refs[:pieces], refs[pieces:]
    place(me_ref[0], piece_refs, slice(None), whole_ref)
    high_ref[...], low_ref[...] = split2(whole_ref[...])


def form_terms(me, pieces):
    rows, cells = pieces[0].shape
    out = jax.ShapeDtypeStruct((rows * len(pieces), cells), BF16)
    scratch = [pltpu.VMEM(out.shape, F32)]
    return call(functools.partial(terms_kernel, len(pieces)), [me[None], *pieces], [out] * 2, scratch)


def solve_kernel(me_ref, mine_ref, other_ref, *refs):
    term_refs, (upper_ref, scores_ref, out_ref, a_ref, inverse_ref, lower_ref, sems) = refs[:-7], refs[-7:]
    half = mine_ref.shape[1]
    first_core = (me_ref[0] & 1) == 0
    mine, other = mine_ref[...], other_ref[...]
    off = jnp.where(first_core, mine[:half], other[:half])
    both = jnp.where(first_core, other[:half], mine[:half])
    scale = 1.0 / mine[half + 1 : half + 2, :]
    row = lax.broadcasted_iota(jnp.int32, (half, half), 0)
    col = lax.broadcasted_iota(jnp.int32, (half, half), 1)
    turned = both.T
    corner = jnp.broadcast_to(mine[half : half + 1, :], (half, half))
    a_ref[:half, :half] = jnp.where(row >= col, both, turned) * scale
    a_ref[half:, half:] = jnp.where(row < col, both, jnp.where(row > col, turned, corner)) * scale
    a_ref[half:, :half] = off * scale
    cholesky_and_inverse(a_ref, inverse_ref, upper_ref, lower_ref)
    high, low = split2(inverse_ref[...])
    copies, at = [], 0
    for high_ref, low_ref in zip(term_refs[::2], term_refs[1::2]):
        for first in range(0, high_ref.shape[1], STEP):
            here = slice(first, min(first + STEP, high_ref.shape[1]))
            there = slice(at + here.start, at + here.stop)
            high_term = high_ref[:, here]
            out_ref[:, there] = dot(high, high_term, NN) + (dot(high, low_ref[:, here], NN) + dot(low, high_term, NN))
            copies.append(pltpu.make_async_copy(out_ref.at[:, there], scores_ref.at[:, there], sems.at[len(copies)]))
            copies[-1].start()
        at += high_ref.shape[1]
    for copy in copies:
        copy.wait()


def solve(me, mine, other, terms):
    order = terms[0].shape[0]
    cells = [term.shape[1] for term in terms[::2]]
    here, square = pl.BlockSpec(memory_space=pltpu.VMEM), (order, order)
    return pl.pallas_call(
        solve_kernel,
        in_specs=[pl.BlockSpec(memory_space=pltpu.SMEM)] + [here] * (2 + len(terms)),
        out_specs=[here, pl.BlockSpec(memory_space=pl.ANY)],
        out_shape=[jax.ShapeDtypeStruct(square, F32), jax.ShapeDtypeStruct((order, sum(cells)), F32)],
        scratch_shapes=[pltpu.VMEM((order, sum(cells)), F32)]
        + [pltpu.VMEM(square, F32)] * 3
        + [pltpu.SemaphoreType.DMA((sum(-(-c // STEP) for c in cells),))],
        compiler_params=pltpu.CompilerParams(vmem_limit_bytes=VMEM_LIMIT),
    )(me[None], mine, other, *terms)


def swap(x, axis, mask):
    return lax.ppermute(x, axis, [(i, i ^ mask) for i in range(lax.axis_size(axis))])


def reduce_over(op, x, axis, first):
    size = lax.axis_size(axis)
    while first < size:
        if 2 * first < size:
            near, far, both = swap(x, axis, first), swap(x, axis, 2 * first), swap(x, axis, 3 * first)
            x = op(op(x, near), op(far, both))
        else:
            x = op(x, swap(x, axis, first))
        first *= 4
    return x


def sum_all(keep, send):
    mine = keep + swap(send, "dev", 1)
    mine = reduce_over(jnp.add, mine, "dev", 2)
    mine = reduce_over(jnp.add, mine, "band", 1)
    return mine, swap(mine, "dev", 1)


def on_device(anomaly, ocean_mask, area_weight):
    size = lax.axis_size("dev")
    me = lax.axis_index("dev")
    cells = anomaly.shape[1] // size
    runs = cells // RUN
    early = runs // 2 * RUN
    others, every = range(1, size), range(size)
    order = sorted(others, key=lambda k: (-(k >> 1).bit_count(), k & 1))
    far, late = order[0], order[-3:-1]
    mask, area = ocean_mask.reshape(-1, LANE), area_weight.reshape(-1, LANE)
    inputs = anomaly, ocean_mask, area_weight
    start_of = lambda k: (me ^ k) * runs
    part = lambda x, k, count=cells: lax.dynamic_slice_in_dim(x, (me ^ k) * cells, count, x.ndim - 1)

    half = lambda k, at: lax.dynamic_slice_in_dim(anomaly, (me ^ k) * cells + at, early, 1)
    raw = swap(half(far, 0), "dev", far)
    source, rank, over, packed = plan_and_pack(start_of(far) + early // RUN, half(far, early), mask, area, swap(area, "dev", 1))
    kept = {far: swap(packed, "dev", far)}
    anomaly, source = lax.optimization_barrier((anomaly, source))
    near = swap(part(anomaly, 1), "dev", 1)
    gate = [swap(over, "dev", 1)]
    for k in order[1:-1]:
        packed = pack_cells(start_of(k), part(anomaly, k), mask, area, source, *gate)
        kept[k] = swap(packed, "dev", k)
        if gate:
            anomaly, ocean_mask, area_weight, source, packed = lax.optimization_barrier((anomaly, ocean_mask, area_weight, source, packed))
            gate = []
    weights = part(area_weight, 0) * part(ocean_mask, 0).astype(F32)
    total = jnp.sum(weights)[None, None]
    root = jnp.sqrt(weights)[None, :]
    own = part(anomaly, 0)
    kept[0] = pack_cells(start_of(0), own, mask, area, source)
    kept[1] = pack_cells(start_of(0), near, mask, area, source)
    kept[far] = jnp.concatenate([pack_cells(start_of(0), raw, mask, area, source), kept[far]], 1)
    pieces = {0: own * root, 1: near * root}
    pieces |= {k: spread(me, rank, kept[k]) for k in others if k not in late and k not in pieces}
    kept[late[-1]], pieces = lax.optimization_barrier((kept[late[-1]], pieces))
    keep, send = form_gram(me, [kept[k] for k in every], total, over)
    mine = keep + swap(send, "dev", 1)
    for k, axis, first in zip(late, ("dev", "band"), (2, 1)):
        mine, rank = lax.optimization_barrier((mine, rank))
        pieces[k] = spread(me, rank, kept[k])
        mine = reduce_over(jnp.add, mine, axis, first)
    terms = form_terms(me, [pieces[k] for k in every])
    mine, terms = lax.optimization_barrier((mine, terms))
    other = swap(mine, "dev", 1)

    def packed_ones(mine, other, terms, inputs):
        return solve(me, mine, other, terms)

    def whole_ones(mine, other, terms, inputs):
        anomaly, ocean_mask, area_weight = inputs
        root = jnp.sqrt(part(area_weight, 0) * part(ocean_mask, 0).astype(F32))[None, :]
        pieces = [part(anomaly, 0)] + [swap(part(anomaly, k), "dev", k) for k in others]
        pieces = [piece * root for piece in pieces]
        return solve(me, *sum_all(*form_gram(me, pieces, total, over)), form_terms(me, pieces))

    return tuple(lax.cond(mine[-1, 0] > 0, whole_ones, packed_ones, mine, other, terms, inputs))


def solution(mesh):
    return jax.shard_map(
        on_device,
        mesh=mesh,
        in_specs=(P("dev", "band"), P("band"), P("band")),
        out_specs=(P(), P(None, ("band", "dev"))),
        check_vma=False,
    )
```

```python
import functools
import jax
import jax.numpy as jnp
from jax import lax
from jax.experimental import pallas as pl
from jax.experimental.pallas import tpu as pltpu
from jax.sharding import PartitionSpec as P

F32, BF16 = jnp.float32, jnp.bfloat16
SUB, LANE = 8, 128
PANEL = 64
NN = (((1,), (0,)), ((), ()))
NT = (((1,), (1,)), ((), ()))
VMEM_LIMIT = 24 * 1024 * 1024
STEP = 512
RUN = 1024
PARTS = RUN // LANE
KEPT = 3 * RUN // 4
STEPS = (RUN - 1).bit_length()


def split2(x):
    high = x.astype(BF16)
    return high, (x - high.astype(F32)).astype(BF16)


def split3(x):
    high = x.astype(BF16)
    rest = x - high.astype(F32)
    middle = rest.astype(BF16)
    return high, middle, (rest - middle.astype(F32)).astype(BF16)


def dot(a, b, dims):
    return lax.dot_general(a, b, dims, preferred_element_type=F32)


def product(a, b, dims):
    a1, a2, a3 = a
    b1, b2, b3 = b
    small = (dot(a1, b3, dims) + dot(a3, b1, dims)) + dot(a2, b2, dims)
    return dot(a1, b1, dims) + ((dot(a1, b2, dims) + dot(a2, b1, dims)) + small)


def tree_sum(terms):
    while len(terms) > 1:
        terms = [sum(terms[i : i + 2][1:], terms[i]) for i in range(0, len(terms), 2)]
    return terms[0]


def row_of(x, k):
    return jnp.broadcast_to(x[k : k + 1, :], (SUB, LANE))


def column_of(x, k):
    return jnp.broadcast_to(x[:, k : k + 1], (SUB, LANE))


def factor_panel(tiles, start):
    tiles = list(tiles)
    count = len(tiles)
    sub = lax.broadcasted_iota(jnp.int32, (SUB, LANE), 0)
    diag = [column_of(tiles[0], start + k) for k in range(SUB)]
    for b in range(count):
        rest = range(b + 1, count)
        cols = {t: [column_of(tiles[t], start + SUB * b + k) for k in range(SUB)] for t in rest}
        ahead = [column_of(tiles[b + 1], start + SUB * (b + 1) + k) for k in range(SUB)] if b + 1 < count else None
        rows = []
        for j in range(SUB):
            inverse = lax.rsqrt(row_of(diag[j], j))
            own = diag[j] * inverse
            spread = {k: row_of(own, k) for k in range(j + 1, SUB)}
            for k in range(j + 1, SUB):
                diag[k] = diag[k] - own * spread[k]
            for t in rest:
                cols[t][j] = cols[t][j] * inverse
                for k in range(j + 1, SUB):
                    cols[t][k] = cols[t][k] - cols[t][j] * spread[k]
            row = row_of(tiles[b], j) * inverse
            tiles[b] = jnp.where(sub == j, row, jnp.where(sub > j, tiles[b] - own * row, tiles[b]))
            rows.append(row)
        if ahead is not None:
            below = cols[b + 1]
            diag = [ahead[k] - tree_sum([below[j] * row_of(below[j], k) for j in range(SUB)]) for k in range(SUB)]
        for t in rest:
            tiles[t] = tiles[t] - tree_sum([cols[t][j] * rows[j] for j in range(SUB)])
    return tiles


def cholesky_and_inverse(a_ref, inverse_ref, upper_ref):
    order = a_ref.shape[0]
    count = order // PANEL
    inverse_ref[...] = jnp.zeros((order, order), F32)
    upper_ref[...] = jnp.zeros((order, order), F32)
    lane = lax.broadcasted_iota(jnp.int32, (SUB, PANEL), 1)
    sub = lax.broadcasted_iota(jnp.int32, (SUB, PANEL), 0)
    block_row = lax.broadcasted_iota(jnp.int32, (PANEL, PANEL), 0)
    block_col = lax.broadcasted_iota(jnp.int32, (PANEL, PANEL), 1)
    block = lambda i: slice(i * PANEL, (i + 1) * PANEL)
    rows_of = lambda terms, first, end: tuple(term[first * PANEL : end * PANEL] for term in terms)
    columns = [a_ref[j * PANEL :, block(j)] for j in range(count)]
    left = [[] for _ in range(count)]
    diag = columns[0][:PANEL]
    for p in range(count):
        tiles = []
        for t in range(PANEL // SUB):
            eye = jnp.where(lane == sub + SUB * t, 1.0, 0.0)
            tiles.append(jnp.concatenate([diag[SUB * t : SUB * t + SUB], eye], 1))
        both = jnp.concatenate(factor_panel(tiles, 0), 0)
        upper_ref[block(p), block(p)] = jnp.where(block_col >= block_row, both[:, :PANEL], 0.0)
        own = both[:, PANEL:]
        own_terms = split3(own)
        below = count - p - 1
        if below:
            lower = product(split3(columns[p][PANEL : 2 * PANEL]), own_terms, NT)
            terms = split3(lower)
            diag = columns[p + 1][:PANEL] - product(terms, terms, NT)
        if below > 1:
            more = product(split3(columns[p][2 * PANEL :]), own_terms, NT)
            lower = jnp.concatenate([lower, more], 0)
            terms = tuple(jnp.concatenate(pair, 0) for pair in zip(terms, split3(more)))
            rest = columns[p + 1][PANEL:] - product(rows_of(terms, 1, below), rows_of(terms, 0, 1), NT)
            columns[p + 1] = jnp.concatenate([columns[p + 1][:PANEL], rest], 0)
            for i in range(1, below):
                columns[p + 1 + i] = columns[p + 1 + i] - product(rows_of(terms, i, below), rows_of(terms, i, i + 1), NT)
        if below:
            upper_ref[block(p), (p + 1) * PANEL :] = lower.T
            for i in range(below):
                left[p + 1 + i].append(lower[block(i)])
        if p:
            behind = product(split3(jnp.concatenate(left[p], 1)), split3(inverse_ref[: p * PANEL, : p * PANEL]), NN)
            inverse_ref[block(p), : p * PANEL] = -product(own_terms, split3(behind), NN)
        inverse_ref[block(p), block(p)] = own


HERE = pl.BlockSpec(memory_space=pltpu.VMEM)
SCALARS = pl.BlockSpec(memory_space=pltpu.SMEM)


def call(kernel, operands, outs, scratch=(), scalars=1, us=1):
    return pl.pallas_call(
        kernel,
        in_specs=[SCALARS] * scalars + [HERE] * (len(operands) - scalars),
        out_specs=[HERE] * len(outs),
        out_shape=outs,
        scratch_shapes=scratch,
        compiler_params=pltpu.CompilerParams(vmem_limit_bytes=VMEM_LIMIT),
        cost_estimate=pl.CostEstimate(flops=us * 1_000_000_000, bytes_accessed=us * 3_600_000, transcendentals=0),
    )(*operands)


def shift_left(parts, by):
    if by >= LANE:
        return parts[by // LANE :] + [jnp.zeros_like(parts[0])] * (by // LANE)
    lane = lax.broadcasted_iota(jnp.int32, parts[0].shape, 1)
    turned = [pltpu.roll(part, LANE - by, 1) for part in parts] + [jnp.zeros_like(parts[0])]
    return [jnp.where(lane < LANE - by, here, after) for here, after in zip(turned, turned[1:])]


def plan(mask_ref, source_ref, rank_ref, over_ref, gap_ref):
    groups = mask_ref.shape[0]
    runs = groups // PARTS
    chunk = min(groups, 2 * LANE)
    bit = lambda keep: jnp.where(keep, 1.0, 0.0).astype(BF16)
    iota = lambda shape, axis: lax.broadcasted_iota(jnp.int32, shape, axis)
    before = bit(iota((LANE, LANE), 0) < iota((LANE, LANE), 1))
    row, col = iota((chunk, chunk), 0), iota((chunk, chunk), 1)
    earlier = bit((row // PARTS == col // PARTS) & (col < row))
    for first in range(0, groups, chunk):
        mask = mask_ref[first : first + chunk, :]
        land = (1 - mask).astype(F32).astype(BF16)
        carried = dot(dot(earlier, land, NN).astype(BF16), jnp.ones((LANE, LANE), BF16), NN)
        gap_ref[first : first + chunk, :] = (dot(land, before, NN) + carried).astype(jnp.int32)
    mask = [mask_ref[pl.ds(p, runs, stride=PARTS), :] for p in range(PARTS)]
    gap = [gap_ref[pl.ds(p, runs, stride=PARTS), :] for p in range(PARTS)]
    last = gap[-1] + (1 - mask[-1])
    count = RUN - jnp.broadcast_to(last[:, LANE - 1 :], (runs, LANE))
    over_ref[...] = jnp.broadcast_to(jnp.max(jnp.where(count > KEPT, 1.0, 0.0), axis=0, keepdims=True), (SUB, LANE))
    lane = iota((runs, LANE), 1)
    for p in range(PARTS):
        rank_ref[p] = jnp.where(mask[p] != 0, lane + p * LANE - gap[p], -1)
    gap = [g * m for g, m in zip(gap, mask)]
    for step in range(STEPS):
        moved = [jnp.where((g & (1 << step)) != 0, g, 0) for g in gap]
        gap = [g - m + a for g, m, a in zip(gap, moved, shift_left(moved, 1 << step))]
    for p in range(PARTS):
        at = lane + p * LANE
        source_ref[p] = jnp.where(at < count, at + gap[p], -1)


def across(ref, at, run):
    return jnp.broadcast_to(ref[at, pl.ds(run, 1), :], (SUB, LANE))


def gathered(parts, index):
    lane, part = index & (LANE - 1), index >> (LANE.bit_length() - 1)
    out = jnp.zeros((SUB, LANE), F32)
    for p, x in parts.items():
        out = jnp.where(part == p, jnp.take_along_axis(x, lane, axis=1, mode="promise_in_bounds"), out)
    return out


def pack(base, x_ref, root_ref, source_ref, out_ref):
    rows, cells = x_ref.shape
    for run in range(cells // RUN):
        index = [across(source_ref, p, base + run) for p in range(KEPT // LANE)]
        for t in range(0, rows, SUB):
            parts = []
            for group in range(run * PARTS, (run + 1) * PARTS):
                root = jnp.broadcast_to(root_ref[group : group + 1, :], (SUB, LANE))
                parts.append(x_ref[t : t + SUB, group * LANE : (group + 1) * LANE] * root)
            for p, lanes in enumerate(index):
                at = run * KEPT + p * LANE
                out_ref[t : t + SUB, at : at + LANE] = gathered({i: parts[i] for i in range(p, PARTS)}, lanes)


def groups_from(base, groups):
    return pl.ds(pl.multiple_of(base * PARTS, PARTS), groups)


def first_kernel(base_ref, x_ref, mask_ref, area_ref, gate_ref, source_ref, rank_ref, over_ref, out_ref, root_ref, gap_ref):
    base = base_ref[0]
    plan(mask_ref, source_ref, rank_ref, over_ref, gap_ref)
    at = groups_from(base, root_ref.shape[0])
    root_ref[...] = jnp.sqrt(area_ref[at, :] * mask_ref[at, :].astype(F32))
    pack(base, x_ref, root_ref, source_ref, out_ref)


def plan_and_pack(base, x, mask, area, gate):
    rows, cells = x.shape
    groups = mask.shape[0]
    moves = jax.ShapeDtypeStruct((PARTS, groups // PARTS, LANE), jnp.int32)
    outs = [moves, moves, jax.ShapeDtypeStruct((SUB, LANE), F32), jax.ShapeDtypeStruct((rows, cells // RUN * KEPT), F32)]
    scratch = [pltpu.VMEM((cells // LANE, LANE), F32), pltpu.VMEM((groups, LANE), jnp.int32)]
    return call(first_kernel, [base[None], x, mask, area, gate], outs, scratch, us=2)


def pack_kernel(base_ref, x_ref, mask_ref, area_ref, source_ref, *refs):
    out_ref, root_ref = refs[-2:]
    base = base_ref[0]
    at = groups_from(base, root_ref.shape[0])
    root_ref[...] = jnp.sqrt(area_ref[at, :] * mask_ref[at, :].astype(F32))
    pack(base, x_ref, root_ref, source_ref, out_ref)


def pack_cells(base, x, mask, area, source, *gate):
    rows, cells = x.shape
    out = jax.ShapeDtypeStruct((rows, cells // RUN * KEPT), F32)
    return call(pack_kernel, [base[None], x, mask, area, source, *gate], [out], [pltpu.VMEM((cells // LANE, LANE), F32)])[0]


def spread_kernel(me_ref, rank_ref, kept_ref, out_ref):
    rows, cells = out_ref.shape
    runs = cells // RUN
    for run in range(runs):
        index = [across(rank_ref, p, me_ref[0] * runs + run) for p in range(PARTS)]
        for t in range(0, rows, SUB):
            parts = [kept_ref[t : t + SUB, first : first + LANE] for first in range(run * KEPT, (run + 1) * KEPT, LANE)]
            for p in range(PARTS):
                first = run * RUN + p * LANE
                out_ref[t : t + SUB, first : first + LANE] = gathered({i: parts[i] for i in range(min(p + 1, len(parts)))}, index[p])


def spread(me, rank, kept):
    out = jax.ShapeDtypeStruct((kept.shape[0], kept.shape[1] // KEPT * RUN), F32)
    return call(spread_kernel, [me[None], rank, kept], [out])[0]


def place(me, refs, at, whole_ref):
    rows = refs[0].shape[0]
    for k, ref in enumerate(refs):
        whole_ref[pl.ds(pl.multiple_of((me ^ k) * rows, rows), rows), at] = ref[:, at]


def products(me, piece_refs, whole_ref):
    main = cross = None
    cells = piece_refs[0].shape[1]
    for first in range(0, cells, STEP):
        at = slice(first, min(first + STEP, cells))
        place(me, piece_refs, at, whole_ref)
        high, low = split2(whole_ref[:, at])
        more_main, more_cross = dot(high, high, NT), dot(high, low, NT)
        main, cross = (main + more_main, cross + more_cross) if first else (more_main, more_cross)
    return main + (cross + cross.T)


def gram_kernel(pieces, me_ref, *refs):
    piece_refs, (total_ref, over_ref, keep_ref, send_ref, whole_ref, sum_ref) = refs[:pieces], refs[pieces:]
    me = me_ref[0]
    sum_ref[...] = products(me, piece_refs, whole_ref)
    half = sum_ref.shape[0] // 2
    row = lax.broadcasted_iota(jnp.int32, (half, half), 0)
    col = lax.broadcasted_iota(jnp.int32, (half, half), 1)
    last = sum_ref[half:, half:]
    both = jnp.where(row >= col, sum_ref[:half, :half], last)
    corner = jnp.sum(jnp.where(row == col, last, 0.0), axis=0, keepdims=True)
    extra_row = lax.broadcasted_iota(jnp.int32, (SUB, half), 0)
    extra = jnp.where(extra_row == 0, jnp.broadcast_to(corner, (SUB, half)), jnp.broadcast_to(total_ref[...], (SUB, half)))
    extra = jnp.where(extra_row == SUB - 1, jnp.broadcast_to(over_ref[:1, :1], (SUB, half)), extra)
    off = sum_ref[half:, :half]
    first_core = (me & 1) == 0
    for ref, is_off in ((keep_ref, first_core), (send_ref, jnp.logical_not(first_core))):
        ref[:half, :] = jnp.where(is_off, off, both)
        ref[half:, :] = extra


def form_gram(me, pieces, total, over):
    rows, cells = pieces[0].shape
    order = rows * len(pieces)
    packed = jax.ShapeDtypeStruct((order // 2 + SUB, order // 2), F32)
    scratch = [pltpu.VMEM((order, cells), F32), pltpu.VMEM((order, order), F32)]
    return call(functools.partial(gram_kernel, len(pieces)), [me[None], *pieces, total, over], [packed] * 2, scratch, us=2)


def terms_kernel(pieces, me_ref, *refs):
    piece_refs, (high_ref, low_ref, whole_ref) = refs[:pieces], refs[pieces:]
    place(me_ref[0], piece_refs, slice(None), whole_ref)
    high_ref[...], low_ref[...] = split2(whole_ref[...])


def form_terms(me, pieces):
    rows, cells = pieces[0].shape
    out = jax.ShapeDtypeStruct((rows * len(pieces), cells), BF16)
    scratch = [pltpu.VMEM(out.shape, F32)]
    return call(functools.partial(terms_kernel, len(pieces)), [me[None], *pieces], [out] * 2, scratch)


def solve_kernel(me_ref, mine_ref, other_ref, *refs):
    term_refs, (upper_ref, scores_ref, out_ref, a_ref, inverse_ref, sems) = refs[:-6], refs[-6:]
    half = mine_ref.shape[1]
    first_core = (me_ref[0] & 1) == 0
    mine, other = mine_ref[...], other_ref[...]
    off = jnp.where(first_core, mine[:half], other[:half])
    both = jnp.where(first_core, other[:half], mine[:half])
    scale = 1.0 / mine[half + 1 : half + 2, :]
    row = lax.broadcasted_iota(jnp.int32, (half, half), 0)
    col = lax.broadcasted_iota(jnp.int32, (half, half), 1)
    turned = both.T
    corner = jnp.broadcast_to(mine[half : half + 1, :], (half, half))
    a_ref[:half, :half] = jnp.where(row >= col, both, turned) * scale
    a_ref[half:, half:] = jnp.where(row < col, both, jnp.where(row > col, turned, corner)) * scale
    a_ref[half:, :half] = off * scale
    cholesky_and_inverse(a_ref, inverse_ref, upper_ref)
    high, low = split2(inverse_ref[...])
    copies, at = [], 0
    for high_ref, low_ref in zip(term_refs[::2], term_refs[1::2]):
        for first in range(0, high_ref.shape[1], STEP):
            here = slice(first, min(first + STEP, high_ref.shape[1]))
            there = slice(at + here.start, at + here.stop)
            high_term = high_ref[:, here]
            out_ref[:, there] = dot(high, high_term, NN) + (dot(high, low_ref[:, here], NN) + dot(low, high_term, NN))
            copies.append(pltpu.make_async_copy(out_ref.at[:, there], scores_ref.at[:, there], sems.at[len(copies)]))
            copies[-1].start()
        at += high_ref.shape[1]
    for copy in copies:
        copy.wait()


def solve(me, mine, other, terms):
    order = terms[0].shape[0]
    cells = [term.shape[1] for term in terms[::2]]
    here, square = pl.BlockSpec(memory_space=pltpu.VMEM), (order, order)
    return pl.pallas_call(
        solve_kernel,
        in_specs=[pl.BlockSpec(memory_space=pltpu.SMEM)] + [here] * (2 + len(terms)),
        out_specs=[here, pl.BlockSpec(memory_space=pl.ANY)],
        out_shape=[jax.ShapeDtypeStruct(square, F32), jax.ShapeDtypeStruct((order, sum(cells)), F32)],
        scratch_shapes=[pltpu.VMEM((order, sum(cells)), F32)]
        + [pltpu.VMEM(square, F32)] * 2
        + [pltpu.SemaphoreType.DMA((sum(-(-c // STEP) for c in cells),))],
        compiler_params=pltpu.CompilerParams(vmem_limit_bytes=VMEM_LIMIT),
    )(me[None], mine, other, *terms)


def swap(x, axis, mask):
    return lax.ppermute(x, axis, [(i, i ^ mask) for i in range(lax.axis_size(axis))])


def reduce_over(op, x, axis, first):
    size = lax.axis_size(axis)
    while first < size:
        if 2 * first < size:
            both, far, near = swap(x, axis, 3 * first), swap(x, axis, 2 * first), swap(x, axis, first)
            x = op(op(x, near), op(far, both))
        else:
            x = op(x, swap(x, axis, first))
        first *= 4
    return x


def sum_all(keep, send):
    mine = keep + swap(send, "dev", 1)
    mine = reduce_over(jnp.add, mine, "dev", 2)
    mine = reduce_over(jnp.add, mine, "band", 1)
    return mine, swap(mine, "dev", 1)


def on_device(anomaly, ocean_mask, area_weight):
    size = lax.axis_size("dev")
    me = lax.axis_index("dev")
    cells = anomaly.shape[1] // size
    runs = cells // RUN
    early = runs // 2 * RUN
    others, every = range(1, size), range(size)
    order = sorted(others, key=lambda k: (-(k >> 1).bit_count(), k & 1))
    far, late = order[0], order[-3:-1]
    mask, area = ocean_mask.reshape(-1, LANE), area_weight.reshape(-1, LANE)
    inputs = anomaly, ocean_mask, area_weight
    start_of = lambda k: (me ^ k) * runs
    part = lambda x, k, count=cells: lax.dynamic_slice_in_dim(x, (me ^ k) * cells, count, x.ndim - 1)

    half = lambda k, at: lax.dynamic_slice_in_dim(anomaly, (me ^ k) * cells + at, early, 1)
    raw = swap(half(far, 0), "dev", far)
    source, rank, over, packed = plan_and_pack(start_of(far) + early // RUN, half(far, early), mask, area, swap(area, "dev", 1))
    kept = {far: swap(packed, "dev", far)}
    anomaly, source = lax.optimization_barrier((anomaly, source))
    near = swap(part(anomaly, 1), "dev", 1)
    gate = [swap(over, "dev", 1)]
    for k in order[1:-1]:
        packed = pack_cells(start_of(k), part(anomaly, k), mask, area, source, *gate)
        kept[k] = swap(packed, "dev", k)
        if gate:
            anomaly, ocean_mask, area_weight, source, packed = lax.optimization_barrier((anomaly, ocean_mask, area_weight, source, packed))
            gate = []
    weights = part(area_weight, 0) * part(ocean_mask, 0).astype(F32)
    total = jnp.sum(weights)[None, None]
    root = jnp.sqrt(weights)[None, :]
    own = part(anomaly, 0)
    kept[0] = pack_cells(start_of(0), own, mask, area, source)
    kept[1] = pack_cells(start_of(0), near, mask, area, source)
    kept[far] = jnp.concatenate([pack_cells(start_of(0), raw, mask, area, source), kept[far]], 1)
    pieces = {0: own * root, 1: near * root}
    pieces |= {k: spread(me, rank, kept[k]) for k in others if k not in late and k not in pieces}
    kept[late[-1]], pieces = lax.optimization_barrier((kept[late[-1]], pieces))
    keep, send = form_gram(me, [kept[k] for k in every], total, over)
    mine = keep + swap(send, "dev", 1)
    for k, axis, first in zip(late, ("dev", "band"), (2, 1)):
        mine, rank = lax.optimization_barrier((mine, rank))
        pieces[k] = spread(me, rank, kept[k])
        mine = reduce_over(jnp.add, mine, axis, first)
    terms = form_terms(me, [pieces[k] for k in every])
    mine, terms = lax.optimization_barrier((mine, terms))
    other = swap(mine, "dev", 1)

    def packed_ones(mine, other, terms, inputs):
        return solve(me, mine, other, terms)

    def whole_ones(mine, other, terms, inputs):
        anomaly, ocean_mask, area_weight = inputs
        root = jnp.sqrt(part(area_weight, 0) * part(ocean_mask, 0).astype(F32))[None, :]
        pieces = [part(anomaly, 0)] + [swap(part(anomaly, k), "dev", k) for k in others]
        pieces = [piece * root for piece in pieces]
        return solve(me, *sum_all(*form_gram(me, pieces, total, over)), form_terms(me, pieces))

    return tuple(lax.cond(mine[-1, 0] > 0, whole_ones, packed_ones, mine, other, terms, inputs))


def solution(mesh):
    return jax.shard_map(
        on_device,
        mesh=mesh,
        in_specs=(P("dev", "band"), P("band"), P("band")),
        out_specs=(P(), P(None, ("band", "dev"))),
        check_vma=False,
    )
```

```python
import functools
import jax
import jax.numpy as jnp
from jax import lax
from jax.experimental import pallas as pl
from jax.experimental.pallas import tpu as pltpu
from jax.sharding import PartitionSpec as P

F32, BF16 = jnp.float32, jnp.bfloat16
SUB, LANE = 8, 128
PANEL = 64
NN = (((1,), (0,)), ((), ()))
NT = (((1,), (1,)), ((), ()))
VMEM_LIMIT = 24 * 1024 * 1024
STEP = 512
RUN = 1024
PARTS = RUN // LANE
KEPT = 3 * RUN // 4
STEPS = (RUN - 1).bit_length()


def split2(x):
    high = x.astype(BF16)
    return high, (x - high.astype(F32)).astype(BF16)


def split3(x):
    high = x.astype(BF16)
    rest = x - high.astype(F32)
    middle = rest.astype(BF16)
    return high, middle, (rest - middle.astype(F32)).astype(BF16)


def dot(a, b, dims):
    return lax.dot_general(a, b, dims, preferred_element_type=F32)


def product(a, b, dims):
    a1, a2, a3 = a
    b1, b2, b3 = b
    small = (dot(a1, b3, dims) + dot(a3, b1, dims)) + dot(a2, b2, dims)
    return dot(a1, b1, dims) + ((dot(a1, b2, dims) + dot(a2, b1, dims)) + small)


def tree_sum(terms):
    while len(terms) > 1:
        terms = [sum(terms[i : i + 2][1:], terms[i]) for i in range(0, len(terms), 2)]
    return terms[0]


def row_of(x, k):
    return jnp.broadcast_to(x[k : k + 1, :], (SUB, LANE))


def column_of(x, k):
    return jnp.broadcast_to(x[:, k : k + 1], (SUB, LANE))


def factor_panel(tiles, start):
    tiles = list(tiles)
    count = len(tiles)
    sub = lax.broadcasted_iota(jnp.int32, (SUB, LANE), 0)
    diag = [column_of(tiles[0], start + k) for k in range(SUB)]
    for b in range(count):
        rest = range(b + 1, count)
        cols = {t: [column_of(tiles[t], start + SUB * b + k) for k in range(SUB)] for t in rest}
        ahead = [column_of(tiles[b + 1], start + SUB * (b + 1) + k) for k in range(SUB)] if b + 1 < count else None
        rows = []
        for j in range(SUB):
            inverse = lax.rsqrt(row_of(diag[j], j))
            own = diag[j] * inverse
            spread = {k: row_of(own, k) for k in range(j + 1, SUB)}
            for k in range(j + 1, SUB):
                diag[k] = diag[k] - own * spread[k]
            for t in rest:
                cols[t][j] = cols[t][j] * inverse
                for k in range(j + 1, SUB):
                    cols[t][k] = cols[t][k] - cols[t][j] * spread[k]
            row = row_of(tiles[b], j) * inverse
            tiles[b] = jnp.where(sub == j, row, jnp.where(sub > j, tiles[b] - own * row, tiles[b]))
            rows.append(row)
        if ahead is not None:
            below = cols[b + 1]
            diag = [ahead[k] - tree_sum([below[j] * row_of(below[j], k) for j in range(SUB)]) for k in range(SUB)]
        for t in rest:
            tiles[t] = tiles[t] - tree_sum([cols[t][j] * rows[j] for j in range(SUB)])
    return tiles


def cholesky_and_inverse(a_ref, inverse_ref, upper_ref, after):
    order = a_ref.shape[0]
    count = order // PANEL
    inverse_ref[...] = jnp.zeros((order, order), F32)
    upper_ref[...] = jnp.zeros((order, order), F32)
    lane = lax.broadcasted_iota(jnp.int32, (SUB, PANEL), 1)
    sub = lax.broadcasted_iota(jnp.int32, (SUB, PANEL), 0)
    block_row = lax.broadcasted_iota(jnp.int32, (PANEL, PANEL), 0)
    block_col = lax.broadcasted_iota(jnp.int32, (PANEL, PANEL), 1)
    block = lambda i: slice(i * PANEL, (i + 1) * PANEL)
    rows_of = lambda terms, first, end: tuple(term[first * PANEL : end * PANEL] for term in terms)
    columns = [a_ref[j * PANEL :, block(j)] for j in range(count)]
    left = [[] for _ in range(count)]
    diag = columns[0][:PANEL]
    for p in range(count):
        tiles = []
        for t in range(PANEL // SUB):
            eye = jnp.where(lane == sub + SUB * t, 1.0, 0.0)
            tiles.append(jnp.concatenate([diag[SUB * t : SUB * t + SUB], eye], 1))
        both = jnp.concatenate(factor_panel(tiles, 0), 0)
        upper_ref[block(p), block(p)] = jnp.where(block_col >= block_row, both[:, :PANEL], 0.0)
        own = both[:, PANEL:]
        own_terms = split3(own)
        below = count - p - 1
        if below:
            lower = product(split3(columns[p][PANEL : 2 * PANEL]), own_terms, NT)
            terms = split3(lower)
            diag = columns[p + 1][:PANEL] - product(terms, terms, NT)
        if below > 1:
            more = product(split3(columns[p][2 * PANEL :]), own_terms, NT)
            lower = jnp.concatenate([lower, more], 0)
            terms = tuple(jnp.concatenate(pair, 0) for pair in zip(terms, split3(more)))
            rest = columns[p + 1][PANEL:] - product(rows_of(terms, 1, below), rows_of(terms, 0, 1), NT)
            columns[p + 1] = jnp.concatenate([columns[p + 1][:PANEL], rest], 0)
            for i in range(1, below):
                columns[p + 1 + i] = columns[p + 1 + i] - product(rows_of(terms, i, below), rows_of(terms, i, i + 1), NT)
        if below:
            upper_ref[block(p), (p + 1) * PANEL :] = lower.T
            for i in range(below):
                left[p + 1 + i].append(lower[block(i)])
        if p:
            behind = product(split3(jnp.concatenate(left[p], 1)), split3(inverse_ref[: p * PANEL, : p * PANEL]), NN)
            inverse_ref[block(p), : p * PANEL] = -product(own_terms, split3(behind), NN)
        inverse_ref[block(p), block(p)] = own
        after((p + 1) * PANEL)


HERE = pl.BlockSpec(memory_space=pltpu.VMEM)
SCALARS = pl.BlockSpec(memory_space=pltpu.SMEM)


def call(kernel, operands, outs, scratch=(), scalars=1, us=1):
    return pl.pallas_call(
        kernel,
        in_specs=[SCALARS] * scalars + [HERE] * (len(operands) - scalars),
        out_specs=[HERE] * len(outs),
        out_shape=outs,
        scratch_shapes=scratch,
        compiler_params=pltpu.CompilerParams(vmem_limit_bytes=VMEM_LIMIT),
        cost_estimate=pl.CostEstimate(flops=us * 1_000_000_000, bytes_accessed=us * 3_600_000, transcendentals=0),
    )(*operands)


def shift_left(parts, by):
    if by >= LANE:
        return parts[by // LANE :] + [jnp.zeros_like(parts[0])] * (by // LANE)
    lane = lax.broadcasted_iota(jnp.int32, parts[0].shape, 1)
    turned = [pltpu.roll(part, LANE - by, 1) for part in parts] + [jnp.zeros_like(parts[0])]
    return [jnp.where(lane < LANE - by, here, after) for here, after in zip(turned, turned[1:])]


def plan(mask_ref, source_ref, rank_ref, over_ref, gap_ref):
    groups = mask_ref.shape[0]
    runs = groups // PARTS
    chunk = min(groups, 2 * LANE)
    bit = lambda keep: jnp.where(keep, 1.0, 0.0).astype(BF16)
    iota = lambda shape, axis: lax.broadcasted_iota(jnp.int32, shape, axis)
    before = bit(iota((LANE, LANE), 0) < iota((LANE, LANE), 1))
    row, col = iota((chunk, chunk), 0), iota((chunk, chunk), 1)
    earlier = bit((row // PARTS == col // PARTS) & (col < row))
    for first in range(0, groups, chunk):
        mask = mask_ref[first : first + chunk, :]
        land = (1 - mask).astype(F32).astype(BF16)
        carried = dot(dot(earlier, land, NN).astype(BF16), jnp.ones((LANE, LANE), BF16), NN)
        gap_ref[first : first + chunk, :] = (dot(land, before, NN) + carried).astype(jnp.int32)
    mask = [mask_ref[pl.ds(p, runs, stride=PARTS), :] for p in range(PARTS)]
    gap = [gap_ref[pl.ds(p, runs, stride=PARTS), :] for p in range(PARTS)]
    last = gap[-1] + (1 - mask[-1])
    count = RUN - jnp.broadcast_to(last[:, LANE - 1 :], (runs, LANE))
    over_ref[...] = jnp.broadcast_to(jnp.max(jnp.where(count > KEPT, 1.0, 0.0), axis=0, keepdims=True), (SUB, LANE))
    lane = iota((runs, LANE), 1)
    for p in range(PARTS):
        rank_ref[p] = jnp.where(mask[p] != 0, lane + p * LANE - gap[p], -1)
    gap = [g * m for g, m in zip(gap, mask)]
    for step in range(STEPS):
        moved = [jnp.where((g & (1 << step)) != 0, g, 0) for g in gap]
        gap = [g - m + a for g, m, a in zip(gap, moved, shift_left(moved, 1 << step))]
    for p in range(PARTS):
        at = lane + p * LANE
        source_ref[p] = jnp.where(at < count, at + gap[p], -1)


def across(ref, at, run):
    return jnp.broadcast_to(ref[at, pl.ds(run, 1), :], (SUB, LANE))


def gathered(parts, index):
    lane, part = index & (LANE - 1), index >> (LANE.bit_length() - 1)
    out = jnp.zeros((SUB, LANE), F32)
    for p, x in parts.items():
        out = jnp.where(part == p, jnp.take_along_axis(x, lane, axis=1, mode="promise_in_bounds"), out)
    return out


def pack(base, x_ref, root_ref, source_ref, out_ref):
    rows, cells = x_ref.shape
    for run in range(cells // RUN):
        index = [across(source_ref, p, base + run) for p in range(KEPT // LANE)]
        for t in range(0, rows, SUB):
            parts = []
            for group in range(run * PARTS, (run + 1) * PARTS):
                root = jnp.broadcast_to(root_ref[group : group + 1, :], (SUB, LANE))
                parts.append(x_ref[t : t + SUB, group * LANE : (group + 1) * LANE] * root)
            for p, lanes in enumerate(index):
                at = run * KEPT + p * LANE
                out_ref[t : t + SUB, at : at + LANE] = gathered({i: parts[i] for i in range(p, PARTS)}, lanes)


def groups_from(base, groups):
    return pl.ds(pl.multiple_of(base * PARTS, PARTS), groups)


def first_kernel(base_ref, x_ref, mask_ref, area_ref, gate_ref, source_ref, rank_ref, over_ref, out_ref, root_ref, gap_ref):
    base = base_ref[0]
    plan(mask_ref, source_ref, rank_ref, over_ref, gap_ref)
    at = groups_from(base, root_ref.shape[0])
    root_ref[...] = jnp.sqrt(area_ref[at, :] * mask_ref[at, :].astype(F32))
    pack(base, x_ref, root_ref, source_ref, out_ref)


def plan_and_pack(base, x, mask, area, gate):
    rows, cells = x.shape
    groups = mask.shape[0]
    moves = jax.ShapeDtypeStruct((PARTS, groups // PARTS, LANE), jnp.int32)
    outs = [moves, moves, jax.ShapeDtypeStruct((SUB, LANE), F32), jax.ShapeDtypeStruct((rows, cells // RUN * KEPT), F32)]
    scratch = [pltpu.VMEM((cells // LANE, LANE), F32), pltpu.VMEM((groups, LANE), jnp.int32)]
    return call(first_kernel, [base[None], x, mask, area, gate], outs, scratch, us=2)


def pack_kernel(base_ref, x_ref, mask_ref, area_ref, source_ref, *refs):
    out_ref, root_ref = refs[-2:]
    base = base_ref[0]
    at = groups_from(base, root_ref.shape[0])
    root_ref[...] = jnp.sqrt(area_ref[at, :] * mask_ref[at, :].astype(F32))
    pack(base, x_ref, root_ref, source_ref, out_ref)


def pack_cells(base, x, mask, area, source, *gate):
    rows, cells = x.shape
    out = jax.ShapeDtypeStruct((rows, cells // RUN * KEPT), F32)
    return call(pack_kernel, [base[None], x, mask, area, source, *gate], [out], [pltpu.VMEM((cells // LANE, LANE), F32)])[0]


def spread_kernel(me_ref, rank_ref, kept_ref, out_ref):
    rows, cells = out_ref.shape
    runs = cells // RUN
    for run in range(runs):
        index = [across(rank_ref, p, me_ref[0] * runs + run) for p in range(PARTS)]
        for t in range(0, rows, SUB):
            parts = [kept_ref[t : t + SUB, first : first + LANE] for first in range(run * KEPT, (run + 1) * KEPT, LANE)]
            for p in range(PARTS):
                first = run * RUN + p * LANE
                out_ref[t : t + SUB, first : first + LANE] = gathered({i: parts[i] for i in range(min(p + 1, len(parts)))}, index[p])


def spread(me, rank, kept):
    out = jax.ShapeDtypeStruct((kept.shape[0], kept.shape[1] // KEPT * RUN), F32)
    return call(spread_kernel, [me[None], rank, kept], [out])[0]


def place(me, refs, at, whole_ref):
    rows = refs[0].shape[0]
    for k, ref in enumerate(refs):
        whole_ref[pl.ds(pl.multiple_of((me ^ k) * rows, rows), rows), at] = ref[:, at]


def products(me, piece_refs, whole_ref):
    main = cross = None
    cells = piece_refs[0].shape[1]
    for first in range(0, cells, STEP):
        at = slice(first, min(first + STEP, cells))
        place(me, piece_refs, at, whole_ref)
        high, low = split2(whole_ref[:, at])
        more_main, more_cross = dot(high, high, NT), dot(high, low, NT)
        main, cross = (main + more_main, cross + more_cross) if first else (more_main, more_cross)
    return main + (cross + cross.T)


def gram_kernel(pieces, me_ref, *refs):
    piece_refs, (total_ref, over_ref, keep_ref, send_ref, whole_ref, sum_ref) = refs[:pieces], refs[pieces:]
    me = me_ref[0]
    sum_ref[...] = products(me, piece_refs, whole_ref)
    half = sum_ref.shape[0] // 2
    row = lax.broadcasted_iota(jnp.int32, (half, half), 0)
    col = lax.broadcasted_iota(jnp.int32, (half, half), 1)
    last = sum_ref[half:, half:]
    both = jnp.where(row >= col, sum_ref[:half, :half], last)
    corner = jnp.sum(jnp.where(row == col, last, 0.0), axis=0, keepdims=True)
    extra_row = lax.broadcasted_iota(jnp.int32, (SUB, half), 0)
    extra = jnp.where(extra_row == 0, jnp.broadcast_to(corner, (SUB, half)), jnp.broadcast_to(total_ref[...], (SUB, half)))
    extra = jnp.where(extra_row == SUB - 1, jnp.broadcast_to(over_ref[:1, :1], (SUB, half)), extra)
    off = sum_ref[half:, :half]
    first_core = (me & 1) == 0
    for ref, is_off in ((keep_ref, first_core), (send_ref, jnp.logical_not(first_core))):
        ref[:half, :] = jnp.where(is_off, off, both)
        ref[half:, :] = extra


def form_gram(me, pieces, total, over):
    rows, cells = pieces[0].shape
    order = rows * len(pieces)
    packed = jax.ShapeDtypeStruct((order // 2 + SUB, order // 2), F32)
    scratch = [pltpu.VMEM((order, cells), F32), pltpu.VMEM((order, order), F32)]
    return call(functools.partial(gram_kernel, len(pieces)), [me[None], *pieces, total, over], [packed] * 2, scratch, us=2)


def terms_kernel(pieces, me_ref, *refs):
    piece_refs, (high_ref, low_ref, whole_ref) = refs[:pieces], refs[pieces:]
    place(me_ref[0], piece_refs, slice(None), whole_ref)
    high_ref[...], low_ref[...] = split2(whole_ref[...])


def form_terms(me, pieces):
    rows, cells = pieces[0].shape
    out = jax.ShapeDtypeStruct((rows * len(pieces), cells), BF16)
    scratch = [pltpu.VMEM(out.shape, F32)]
    return call(functools.partial(terms_kernel, len(pieces)), [me[None], *pieces], [out] * 2, scratch)


def solve_kernel(me_ref, mine_ref, other_ref, *refs):
    term_refs, (upper_ref, scores_ref, out_ref, a_ref, inverse_ref, sems) = refs[:-6], refs[-6:]
    half = mine_ref.shape[1]
    first_core = (me_ref[0] & 1) == 0
    mine, other = mine_ref[...], other_ref[...]
    off = jnp.where(first_core, mine[:half], other[:half])
    both = jnp.where(first_core, other[:half], mine[:half])
    scale = 1.0 / mine[half + 1 : half + 2, :]
    row = lax.broadcasted_iota(jnp.int32, (half, half), 0)
    col = lax.broadcasted_iota(jnp.int32, (half, half), 1)
    turned = both.T
    corner = jnp.broadcast_to(mine[half : half + 1, :], (half, half))
    a_ref[:half, :half] = jnp.where(row >= col, both, turned) * scale
    a_ref[half:, half:] = jnp.where(row < col, both, jnp.where(row > col, turned, corner)) * scale
    a_ref[half:, :half] = off * scale
    high_ref, low_ref = term_refs
    copies = []

    def form_scores(rows):
        if rows % half:
            return
        high, low = split2(inverse_ref[rows - half : rows, :rows])
        for first in range(0, high_ref.shape[1], STEP):
            at = (slice(rows - half, rows), slice(first, min(first + STEP, high_ref.shape[1])))
            high_term, low_term = high_ref[:rows, at[1]], low_ref[:rows, at[1]]
            out_ref[at] = dot(high, high_term, NN) + (dot(high, low_term, NN) + dot(low, high_term, NN))
            copies.append(pltpu.make_async_copy(out_ref.at[at], scores_ref.at[at], sems.at[len(copies)]))
            copies[-1].start()

    cholesky_and_inverse(a_ref, inverse_ref, upper_ref, form_scores)
    for copy in copies:
        copy.wait()


def solve(me, mine, other, terms):
    order = terms[0].shape[0]
    cells = [term.shape[1] for term in terms[::2]]
    here, square = pl.BlockSpec(memory_space=pltpu.VMEM), (order, order)
    return pl.pallas_call(
        solve_kernel,
        in_specs=[pl.BlockSpec(memory_space=pltpu.SMEM)] + [here] * (2 + len(terms)),
        out_specs=[here, pl.BlockSpec(memory_space=pl.ANY)],
        out_shape=[jax.ShapeDtypeStruct(square, F32), jax.ShapeDtypeStruct((order, sum(cells)), F32)],
        scratch_shapes=[pltpu.VMEM((order, sum(cells)), F32)]
        + [pltpu.VMEM(square, F32)] * 2
        + [pltpu.SemaphoreType.DMA((2 * sum(-(-c // STEP) for c in cells),))],
        compiler_params=pltpu.CompilerParams(vmem_limit_bytes=VMEM_LIMIT),
    )(me[None], mine, other, *terms)


def swap(x, axis, mask):
    return lax.ppermute(x, axis, [(i, i ^ mask) for i in range(lax.axis_size(axis))])


def reduce_over(op, x, axis, first):
    size = lax.axis_size(axis)
    while first < size:
        if 2 * first < size:
            both, far, near = swap(x, axis, 3 * first), swap(x, axis, 2 * first), swap(x, axis, first)
            x = op(op(x, near), op(far, both))
        else:
            x = op(x, swap(x, axis, first))
        first *= 4
    return x


def sum_all(keep, send):
    mine = keep + swap(send, "dev", 1)
    mine = reduce_over(jnp.add, mine, "dev", 2)
    mine = reduce_over(jnp.add, mine, "band", 1)
    return mine, swap(mine, "dev", 1)


def on_device(anomaly, ocean_mask, area_weight):
    size = lax.axis_size("dev")
    me = lax.axis_index("dev")
    cells = anomaly.shape[1] // size
    runs = cells // RUN
    early = runs // 2 * RUN
    others, every = range(1, size), range(size)
    order = sorted(others, key=lambda k: (-(k >> 1).bit_count(), k & 1))
    far, late = order[0], order[-3:-1]
    mask, area = ocean_mask.reshape(-1, LANE), area_weight.reshape(-1, LANE)
    inputs = anomaly, ocean_mask, area_weight
    start_of = lambda k: (me ^ k) * runs
    part = lambda x, k, count=cells: lax.dynamic_slice_in_dim(x, (me ^ k) * cells, count, x.ndim - 1)

    half = lambda k, at: lax.dynamic_slice_in_dim(anomaly, (me ^ k) * cells + at, early, 1)
    raw = swap(half(far, 0), "dev", far)
    source, rank, over, packed = plan_and_pack(start_of(far) + early // RUN, half(far, early), mask, area, swap(area, "dev", 1))
    kept = {far: swap(packed, "dev", far)}
    anomaly, source = lax.optimization_barrier((anomaly, source))
    near = swap(part(anomaly, 1), "dev", 1)
    gate = [swap(over, "dev", 1)]
    for k in order[1:-1]:
        packed = pack_cells(start_of(k), part(anomaly, k), mask, area, source, *gate)
        kept[k] = swap(packed, "dev", k)
        if gate:
            anomaly, ocean_mask, area_weight, source, packed = lax.optimization_barrier((anomaly, ocean_mask, area_weight, source, packed))
            gate = []
    weights = part(area_weight, 0) * part(ocean_mask, 0).astype(F32)
    total = jnp.sum(weights)[None, None]
    root = jnp.sqrt(weights)[None, :]
    own = part(anomaly, 0)
    kept[0] = pack_cells(start_of(0), own, mask, area, source)
    kept[1] = pack_cells(start_of(0), near, mask, area, source)
    kept[far] = jnp.concatenate([pack_cells(start_of(0), raw, mask, area, source), kept[far]], 1)
    pieces = {0: own * root, 1: near * root}
    pieces |= {k: spread(me, rank, kept[k]) for k in others if k not in late and k not in pieces}
    kept[late[-1]], pieces = lax.optimization_barrier((kept[late[-1]], pieces))
    keep, send = form_gram(me, [kept[k] for k in every], total, over)
    mine = keep + swap(send, "dev", 1)
    for k, axis, first in zip(late, ("dev", "band"), (2, 1)):
        mine, rank = lax.optimization_barrier((mine, rank))
        pieces[k] = spread(me, rank, kept[k])
        mine = reduce_over(jnp.add, mine, axis, first)
    terms = form_terms(me, [pieces[k] for k in every])
    mine, terms = lax.optimization_barrier((mine, terms))
    other = swap(mine, "dev", 1)

    def packed_ones(mine, other, terms, inputs):
        return solve(me, mine, other, terms)

    def whole_ones(mine, other, terms, inputs):
        anomaly, ocean_mask, area_weight = inputs
        root = jnp.sqrt(part(area_weight, 0) * part(ocean_mask, 0).astype(F32))[None, :]
        pieces = [part(anomaly, 0)] + [swap(part(anomaly, k), "dev", k) for k in others]
        pieces = [piece * root for piece in pieces]
        return solve(me, *sum_all(*form_gram(me, pieces, total, over)), form_terms(me, pieces))

    return tuple(lax.cond(mine[-1, 0] > 0, whole_ones, packed_ones, mine, other, terms, inputs))


def solution(mesh):
    return jax.shard_map(
        on_device,
        mesh=mesh,
        in_specs=(P("dev", "band"), P("band"), P("band")),
        out_specs=(P(), P(None, ("band", "dev"))),
        check_vma=False,
    )
```
